128 devices in a mesh: row: 8 (over x_lo, z), col: 16 (over y, x_hi, core).
Axes of the slice: x: 4 (x_hi: 2, x_lo: 2; x = x_hi * 2 + x_lo), y: 4, z: 4, core: 2. Of those that a mesh axis runs over, the one named last changes fastest.
Arguments:
- pair_act: bfloat16 [2048, 2048, 128], P('row', 'col'), may hold values from -6 to 6
- atom_act: bfloat16 [16384, 128], P(('row', 'col')), may hold values from -6 to 6
- atom_token: int32 [16384], P(('row', 'col')), may hold values from 0 to 2047, as said below
- atom_gain: float32 [128], replicated, may hold values from 0.1 to 1.9
- w_attn: bfloat16 [128, 512], replicated, may hold values from -0.5 to 0.5
- w_out: bfloat16 [128, 128], replicated, may hold values from -0.5 to 0.5
- w_bias: bfloat16 [128, 4], replicated, may hold values from -9.722718 to 9.722718
- w_trans_in: bfloat16 [128, 1024], replicated, may hold values from -0.5 to 0.5
- w_trans_out: bfloat16 [512, 128], replicated, may hold values from -0.25 to 0.25
- w_agg: bfloat16 [128, 384], replicated, may hold values from -0.5 to 0.5
- w_single: bfloat16 [384, 256], replicated, may hold values from -0.3125 to 0.3125
Outputs:
- atom_out: bfloat16 [16384, 128], P(('row', 'col'))
- token_single: bfloat16 [2048, 384], P(('row', 'col'))
- pair_out: bfloat16 [2048, 2048, 128], P('row', 'col')
The draws below stay inside these ranges and needn't reach their ends.
Inputs may be any that keep to these rules, and one draw needn't show every extreme that they name: `atom_token`: non-decreasing; token 0 begins at atom 0, and the first atom of every other token t lies between atoms 8 t and 8 t + 4, and between 8 t + 1 and 8 t + 4 where t is a positive multiple of 16; so every token has 4 to 12 atoms, atom i belongs to a token from 16 * (i // 128) - 1 to 16 * (i // 128) + 15, and a query atom and each of its keys belong to tokens at most 10 apart.
All inputs are finite; a program needn't handle non-finite values.
Results may differ from the reference program's by a relative error of at most 0.0075.
Values may be sent and summed in bfloat16 or wider, within the bound.
No kernel may reach another device: no remote copies, remote signals or barrier semaphores. Data moves between devices by JAX's collectives and lax.ppermute only.
A program may use at most 128 MiB of HBM per device.

```python
import math
import jax
import jax.numpy as jnp
from jax import lax

CP = 128
CS = 384
CA = 128
H = 4
TF = 512
QB = 32
KW = 128
DH = 32
TOK_DEV = 16
SPAN = 10
NATOM = 16384
TOK = 2048


def draw_atom_token(key, part):
    key = jax.random.fold_in(key, 7)
    levels = jax.random.randint(key, (TOK,), 0, 5)
    levels = levels.at[0].set(4).at[1].set(0).at[2].set(4)
    levels = levels.at[QB // 8 + SPAN - 1].set(4).at[QB // 8].set(0)
    token_ids = jnp.arange(TOK, dtype=jnp.int32)
    device_first = (token_ids % TOK_DEV == 0) & (token_ids > 0)
    levels = jnp.where(device_first, levels % 4, levels)
    counts = 8 + levels - jnp.roll(levels, -1)
    ends = jnp.cumsum(counts)
    atoms = jnp.arange(NATOM, dtype=jnp.int32)
    return jnp.searchsorted(ends, atoms, side='right').astype(jnp.int32)


def draw_w_bias(key, part):
    key = jax.random.fold_in(key, 11)
    first = jax.random.fold_in(key, 0)
    base = jnp.clip(jax.random.normal(first, (CP, H), jnp.float32), -4.0, 4.0)
    return (base * CP ** (-0.5)).astype(jnp.bfloat16)


def block_scale(key, shape, cuts, least, top_value):
    loudness, own = 1.0, jax.random.fold_in(key, 6)
    for dim, parts in cuts:
        draws = jnp.exp(jax.random.uniform(jax.random.fold_in(own, dim), (parts,), jnp.float32, least / len(cuts), top_value / len(cuts)))
        loudness = loudness * jnp.repeat(draws, shape[dim] // parts).reshape([-1 if axis == dim else 1 for axis in range(len(shape))])
    return loudness


def bell_draw(rng, extent, width, reach, cuts=(), kind=jnp.bfloat16):
    level = block_scale(rng, extent, cuts, -0.22, 0.18) if cuts else 1.0
    array = jax.random.normal(rng, extent, jnp.float32) * width * level
    return jnp.minimum(jnp.maximum(array, -reach), reach).astype(kind)


def setup_inputs(seed: int = 0) -> dict:
    keys = jax.random.split(jax.random.key(seed), 12)
    return {
        "pair_act": bell_draw(keys[0], (TOK, TOK, CP), 1.0, 6.0, ((0, 8), (1, 16))),
        "atom_act": bell_draw(keys[1], (NATOM, CA), 1.0, 6.0, ((0, 128),)),
        "atom_token": draw_atom_token(jax.random.fold_in(keys[11], 71), 0),
        "atom_gain": jnp.clip(1.0 + 0.18 * jax.random.normal(keys[3], (CA,), jnp.float32), 0.1, 1.9),
        "w_attn": bell_draw(keys[4], (CA, 4 * CA), CA ** -0.5, 0.5),
        "w_out": bell_draw(keys[5], (CA, CA), CA ** -0.5, 0.5),
        "w_bias": draw_w_bias(jax.random.fold_in(keys[11], 71), 0),
        "w_trans_in": bell_draw(keys[7], (CP, 2 * TF), CP ** -0.5, 0.5),
        "w_trans_out": bell_draw(keys[8], (TF, CP), TF ** -0.5, 0.25),
        "w_agg": bell_draw(keys[9], (CA, CS), CA ** -0.5, 0.5),
        "w_single": bell_draw(keys[10], (CS, 2 * CP), CS ** -0.5, 0.3125),
    }


def normalize(values):
    centre = values - lax.optimization_barrier(jnp.mean(values, axis=-1, keepdims=True))
    spread = lax.optimization_barrier(jnp.mean(centre * centre, axis=-1, keepdims=True))
    return centre * lax.rsqrt(spread + 1e-05)

def reference(pair_act, atom_act, atom_token, atom_gain, w_attn, w_out, w_bias, w_trans_in, w_trans_out, w_agg, w_single):
    row_blocks = pair_act.reshape(TOK // TOK_DEV, TOK_DEV, TOK, CP)

    def bias_block(pair_rows):
        flat_rows = pair_rows.reshape(TOK_DEV * TOK, CP)
        normed = normalize(flat_rows.astype(jnp.float32)).astype(jnp.bfloat16)
        biases = jnp.dot(normed, w_bias, preferred_element_type=jnp.float32).astype(jnp.bfloat16)
        return biases.reshape(TOK_DEV, TOK, H)
    pair_bias = lax.map(bias_block, row_blocks).reshape(TOK, TOK, H)
    atom_float = atom_act.astype(jnp.float32)
    normed_atoms = (normalize(atom_float) * atom_gain).astype(jnp.bfloat16)
    projected = jnp.dot(normed_atoms, w_attn, preferred_element_type=jnp.float32)
    queries = projected[:, :CA].astype(jnp.bfloat16)
    key_rows = projected[:, CA:2 * CA].astype(jnp.bfloat16)
    value_rows = projected[:, 2 * CA:3 * CA].astype(jnp.bfloat16)
    gating = jax.nn.sigmoid(projected[:, 3 * CA:])
    key_margin = (KW - QB) // 2
    blocks = NATOM // QB
    key_index = (jnp.arange(blocks, dtype=jnp.int32) * QB - key_margin)[:, None] + jnp.arange(KW, dtype=jnp.int32)[None, :]
    usable = (key_index >= 0) & (key_index < NATOM)
    clipped = jnp.clip(key_index, 0, NATOM - 1)
    query_heads = queries.reshape(blocks, QB, H, DH).astype(jnp.float32)
    key_heads = key_rows[clipped].reshape(blocks, KW, H, DH).astype(jnp.float32)
    value_heads = value_rows[clipped].reshape(blocks, KW, H, DH).astype(jnp.float32)
    scores = jnp.einsum('bqhd,bkhd->bhqk', query_heads, key_heads) * (1.0 / math.sqrt(DH))
    query_token = atom_token.reshape(blocks, QB)
    key_token = atom_token[clipped]
    key_bias = pair_bias[query_token[:, :, None], key_token[:, None, :]].astype(jnp.float32)
    scores = scores + jnp.transpose(key_bias, (0, 3, 1, 2))
    scores = jnp.where(usable[:, None, None, :], scores, -jnp.inf)
    row_max = lax.optimization_barrier(jnp.max(scores, axis=-1, keepdims=True))
    exponent = jnp.exp(scores - row_max)
    weights = (exponent / lax.optimization_barrier(jnp.sum(exponent, axis=-1, keepdims=True))).astype(jnp.bfloat16)
    attended = jnp.einsum('bhqk,bkhd->bqhd', weights.astype(jnp.float32), value_heads).reshape(NATOM, CA)
    attended = (gating * attended).astype(jnp.bfloat16)
    atom_out = (atom_float + jnp.dot(attended, w_out, preferred_element_type=jnp.float32)).astype(jnp.bfloat16)
    features = jax.nn.relu(jnp.dot(atom_out, w_agg, preferred_element_type=jnp.float32))
    token_totals = jax.ops.segment_sum(features, atom_token, num_segments=TOK)
    counts = jax.ops.segment_sum(jnp.ones((NATOM,), jnp.float32), atom_token, num_segments=TOK)
    token_single = (token_totals / counts[:, None]).astype(jnp.bfloat16)
    singles = jnp.dot(token_single, w_single, preferred_element_type=jnp.float32)
    row_singles = singles[:, :CP].astype(jnp.bfloat16)
    col_singles = singles[:, CP:].astype(jnp.bfloat16)

    def update_block(pieces):
        pair_rows, row_extra = pieces
        flat_rows = pair_rows.reshape(TOK_DEV * TOK, CP)
        normed = normalize(flat_rows.astype(jnp.float32)).astype(jnp.bfloat16)
        hidden_pre = jnp.dot(normed, w_trans_in, preferred_element_type=jnp.float32)
        hidden = (jax.nn.silu(hidden_pre[:, :TF]) * hidden_pre[:, TF:]).astype(jnp.bfloat16)
        updated = flat_rows.astype(jnp.float32) + jnp.dot(hidden, w_trans_out, preferred_element_type=jnp.float32)
        updated = updated.reshape(TOK_DEV, TOK, CP) + row_extra.astype(jnp.float32)[:, None, :]
        updated = updated + col_singles.astype(jnp.float32)[None, :, :]
        return updated.astype(jnp.bfloat16)
    pair_out = lax.map(update_block, (row_blocks, row_singles.reshape(TOK // TOK_DEV, TOK_DEV, CP)))
    return (atom_out, token_single, pair_out.reshape(TOK, TOK, CP))
```

```python
import functools
import math

import jax
import jax.numpy as jnp
from jax import lax
from jax.experimental import pallas as pl
from jax.experimental.pallas import tpu as pltpu
from jax.sharding import PartitionSpec as P

SPAN = 10
QB = 32
KW = 128
TOK_DEV = 16
BELOW = (KW - QB) // 2
ABOVE = KW - BELOW
WINDOW = 64
GROUPS = 9
BAND_ROWS = 32
VMEM_BYTES = 56 * 1024 * 1024


def normalize(values):
    centre = values - jnp.mean(values, axis=-1, keepdims=True)
    spread = jnp.mean(centre * centre, axis=-1, keepdims=True)
    return centre * lax.rsqrt(spread + 1e-05)


def dot(a, b, **kw):
    return jnp.dot(a, b, preferred_element_type=jnp.float32, **kw)


def dot_nt(a, b):
    return lax.dot_general(a, b, (((1,), (1,)), ((), ())), preferred_element_type=jnp.float32)


def band_kernel(place_ref, pair_ref, weight_ref, out_ref, cells, rows_scr, sems):
    row, col = place_ref[0], place_ref[1]
    shift = col - 2 * row
    first = jnp.clip(8 * shift - 1, 0, 7)
    pieces = WINDOW // 16
    copies = []
    for j in range(GROUPS):
        group = first + j
        start = group - 8 * shift - 1
        mine = []
        for t in range(pieces):
            piece = jnp.clip(start + t, 0, 7)
            copy = pltpu.make_async_copy(
                pair_ref.at[
                    pl.ds(pl.multiple_of(group * 16, 16), 16),
                    pl.ds(pl.multiple_of(piece * 16, 16), 16),
                    :,
                ],
                cells.at[j, :, pl.ds(16 * t, 16), :],
                sems.at[j, t],
            )
            copy.start()
            mine.append(copy)
        copies.append(mine)
    out_ref[...] = jnp.zeros_like(out_ref)
    lane_piece = (lax.broadcasted_iota(jnp.int32, (BAND_ROWS, 128), 1) % WINDOW) // 16
    for j in range(GROUPS):
        group = first + j
        start = group - 8 * shift - 1
        for copy in copies[j]:
            copy.wait()
        flat = cells[j].reshape(16 * WINDOW, 128)
        normed = normalize(flat.astype(jnp.float32)).astype(jnp.bfloat16)
        biases = dot_nt(weight_ref[...], normed)
        for i in range(8):
            rows_scr[j, 4 * i : 4 * i + 4, :] = biases[0:4, 128 * i : 128 * (i + 1)]
        at = start + lane_piece
        kept = jnp.where((at >= 0) & (at <= 7), rows_scr[j], 0.0)
        out_ref[pl.ds(group, 1)] = kept.astype(jnp.bfloat16)[None]


def band_biases(place, pair_act, w_bias):
    n_col = 16
    weight = jnp.zeros((16, 128), jnp.bfloat16).at[:4].set(w_bias.T)
    return pl.pallas_call(
        band_kernel,
        in_specs=[
            pl.BlockSpec(memory_space=pltpu.SMEM),
            pl.BlockSpec(memory_space=pl.ANY),
            pl.BlockSpec(memory_space=pltpu.VMEM),
        ],
        out_specs=pl.BlockSpec(memory_space=pltpu.VMEM),
        out_shape=jax.ShapeDtypeStruct((n_col, BAND_ROWS, 128), jnp.bfloat16),
        scratch_shapes=[
            pltpu.VMEM((GROUPS, 16, WINDOW, 128), jnp.bfloat16),
            pltpu.VMEM((GROUPS, BAND_ROWS, 128), jnp.float32),
            pltpu.SemaphoreType.DMA((GROUPS, WINDOW // 16)),
        ],
        cost_estimate=pl.CostEstimate(flops=10**9, bytes_accessed=3 * 10**6, transcendentals=0),
        compiler_params=pltpu.CompilerParams(vmem_limit_bytes=VMEM_BYTES),
        name="band",
    )(place, pair_act, weight)


def atom_kernel(
    place_ref, below_ref, own_ref, above_ref, tok_ref, band_ref, gain_ref, wattn_ref, wout_ref,
    wagg_ref, wsingle_ref, atom_out_ref, next_out_ref, token_ref, singles_ref,
    wide, q_scr, k_scr, v_scr, gate_scr,
):
    flat = place_ref[2]
    atoms = own_ref.shape[0]
    heads = 4
    n_query = atoms + QB
    total = place_ref[3]
    wide[0:BELOW, :] = below_ref[0:BELOW, :].astype(jnp.float32)
    wide[BELOW : BELOW + atoms, :] = own_ref[...].astype(jnp.float32)
    wide[BELOW + atoms :, :] = above_ref[0:ABOVE, :].astype(jnp.float32)
    normed = (normalize(wide[...]) * gain_ref[...]).astype(jnp.bfloat16)
    projected = dot(normed, wattn_ref[...])
    q_scr[...] = projected[BELOW : BELOW + n_query, 0:128].astype(jnp.bfloat16)
    k_scr[...] = projected[:, 128:256].astype(jnp.bfloat16)
    v_scr[...] = projected[:, 256:384].astype(jnp.bfloat16)
    gate_scr[...] = jax.nn.sigmoid(projected[BELOW : BELOW + n_query, 384:512])

    tok_own = tok_ref[0:1, :].astype(jnp.float32)
    tok_below = below_ref[BELOW : BELOW + 16, :].astype(jnp.float32)[0:1] - TOK_DEV
    tok_above = above_ref[ABOVE : ABOVE + 16, :].astype(jnp.float32)[0:1] + TOK_DEV
    lane = lax.broadcasted_iota(jnp.int32, (8, 128), 1)
    rolled_own = pltpu.roll(jnp.broadcast_to(tok_own, (8, 128)), BELOW, 1)
    rolled_below = pltpu.roll(jnp.broadcast_to(tok_below, (8, 128)), BELOW, 1)
    rolled_above = pltpu.roll(jnp.broadcast_to(tok_above, (8, 128)), BELOW, 1)
    key_tok = jnp.concatenate(
        [
            jnp.where(lane < BELOW, rolled_below, rolled_own)[0:1],
            jnp.where(lane < BELOW, rolled_own, rolled_above)[0:1],
        ],
        axis=1,
    )
    col_own = jnp.transpose(jnp.broadcast_to(tok_own, (128, 128)))
    col_above = jnp.transpose(jnp.broadcast_to(tok_above, (128, 128)))

    band = jnp.sum(band_ref[...].astype(jnp.float32), axis=0)
    half = lax.broadcasted_iota(jnp.int32, (BAND_ROWS, 128), 1) < WINDOW
    band = jnp.concatenate([jnp.where(half, band, 0.0), jnp.where(half, 0.0, band)], axis=0)
    slot = (lax.broadcasted_iota(jnp.int32, (128, 256), 0) % WINDOW - 16).astype(jnp.float32)
    pick_key = (slot == key_tok).astype(jnp.bfloat16)
    spread = dot(band.astype(jnp.bfloat16), pick_key).astype(jnp.bfloat16)

    row_head = lax.broadcasted_iota(jnp.int32, (128, 128), 0) // QB
    lane_head = lax.broadcasted_iota(jnp.int32, (128, 128), 1) // 32
    own_head = row_head == lane_head
    entry = lax.broadcasted_iota(jnp.int32, (128, WINDOW), 1)
    entry_tok = (2 * ((entry % 32) // 4) + entry // 32).astype(jnp.float32)
    entry_head = entry % 4 == lax.broadcasted_iota(jnp.int32, (128, WINDOW), 0) // QB
    key_lane = lax.broadcasted_iota(jnp.int32, (128, KW), 1)
    for b in range(n_query // QB):
        at = b * QB
        queries = q_scr[at : at + QB, :]
        stacked = jnp.where(own_head, jnp.concatenate([queries] * heads, axis=0), 0)
        keys = k_scr[at : at + KW, :]
        tok_col = col_own[at : at + QB, 0:WINDOW] if at < atoms else col_above[0:QB, 0:WINDOW]
        pick = (jnp.concatenate([tok_col] * heads, axis=0) == entry_tok) & entry_head
        bias = dot(pick.astype(jnp.bfloat16), spread[:, at : at + KW])
        scores = dot_nt(stacked, keys) * (1.0 / math.sqrt(32)) + bias
        key_index = flat * atoms - BELOW + at + key_lane
        scores = jnp.where((key_index >= 0) & (key_index < total), scores, -jnp.inf)
        exponent = jnp.exp(scores - jnp.max(scores, axis=-1, keepdims=True))
        weights = (exponent / jnp.sum(exponent, axis=-1, keepdims=True)).astype(jnp.bfloat16)
        mixed = jnp.where(own_head, dot(weights, v_scr[at : at + KW, :]), 0.0)
        mixed = (mixed[0:32] + mixed[32:64]) + (mixed[64:96] + mixed[96:128])
        gate_scr[at : at + QB, :] = gate_scr[at : at + QB, :] * mixed
    attended = gate_scr[...].astype(jnp.bfloat16)
    atom_out = (wide[BELOW : BELOW + n_query, :] + dot(attended, wout_ref[...])).astype(
        jnp.bfloat16
    )
    atom_out_ref[...] = atom_out[0:atoms]
    next_out_ref[...] = atom_out[atoms : atoms + 16]
    features = jnp.maximum(dot(atom_out, wagg_ref[...]), 0.0)
    tokens = lax.broadcasted_iota(jnp.int32, (TOK_DEV, 128), 0).astype(jnp.float32)
    member = (tok_own == tokens).astype(jnp.float32)
    member_next = ((tok_above == tokens) & (key_lane[0:TOK_DEV] < QB)).astype(jnp.float32)[:, 0:QB]
    counts = jnp.sum(member, axis=1, keepdims=True) + jnp.sum(member_next, axis=1, keepdims=True)
    totals = dot(member, features[0:atoms], precision=lax.Precision.HIGHEST) + dot(
        member_next, features[atoms:], precision=lax.Precision.HIGHEST
    )
    token_single = (totals / counts).astype(jnp.bfloat16)
    token_ref[...] = token_single
    singles_ref[...] = dot(token_single, wsingle_ref[...]).astype(jnp.bfloat16)


def atom_part(place, below, own, above, tok_rows, band, atom_gain, w_attn, w_out, w_agg, w_single):
    atoms = own.shape[0]
    vmem = pl.BlockSpec(memory_space=pltpu.VMEM)
    return pl.pallas_call(
        atom_kernel,
        in_specs=[pl.BlockSpec(memory_space=pltpu.SMEM)] + [vmem] * 10,
        out_specs=[vmem] * 4,
        out_shape=[
            jax.ShapeDtypeStruct((atoms, 128), jnp.bfloat16),
            jax.ShapeDtypeStruct((16, 128), jnp.bfloat16),
            jax.ShapeDtypeStruct((TOK_DEV, 384), jnp.bfloat16),
            jax.ShapeDtypeStruct((TOK_DEV, 256), jnp.bfloat16),
        ],
        scratch_shapes=[
            pltpu.VMEM((atoms + KW, 128), jnp.float32),
            pltpu.VMEM((atoms + QB, 128), jnp.bfloat16),
            pltpu.VMEM((atoms + KW, 128), jnp.bfloat16),
            pltpu.VMEM((atoms + KW, 128), jnp.bfloat16),
            pltpu.VMEM((atoms + QB, 128), jnp.float32),
        ],
        cost_estimate=pl.CostEstimate(flops=10**9, bytes_accessed=10**6, transcendentals=10**5),
        compiler_params=pltpu.CompilerParams(vmem_limit_bytes=VMEM_BYTES),
        name="atoms",
    )(place, below, own, above, tok_rows, band, atom_gain, w_attn, w_out, w_agg, w_single)


def transition(cells, w_in, w_out):
    width = w_out.shape[0]
    wide = cells.astype(jnp.float32)
    hidden = dot(normalize(wide).astype(jnp.bfloat16), w_in)
    gate = hidden[:, :width].astype(jnp.bfloat16)
    up = hidden[:, width:].astype(jnp.bfloat16)
    return wide + dot((gate + gate * jnp.tanh(gate)) * up, w_out)


ROWS = 16
SUB = 512
PARTS = 4


def part_kernel(rows_n, pair_ref, w_in_ref, w_out_ref, *refs):
    out_ref = refs[-1]
    cols = pair_ref.shape[1]
    step = SUB // cols
    for i in range(rows_n // step):
        cells = pair_ref[i * step : (i + 1) * step].reshape(SUB, 128)
        moved = transition(cells, w_in_ref[...], w_out_ref[...])
        out_ref[i * step : (i + 1) * step] = moved.astype(jnp.bfloat16).reshape(step, cols, 128)


def pair_part(pair_act, w_in, w_out, part, first, count, earlier, after):
    rows, cols, width = pair_act.shape
    block = (ROWS, cols, width)
    whole = pl.BlockSpec(memory_space=pltpu.VMEM)
    anywhere = pl.BlockSpec(memory_space=pl.ANY)
    args = [pair_act, w_in, w_out]
    specs = [pl.BlockSpec(block, lambda i: (PARTS * (first + i) + part, 0, 0)), whole, whole]
    aliases = {}
    if earlier is not None:
        aliases = {len(args): 0}
        args.append(earlier)
        specs.append(anywhere)
    for value in after:
        args.append(value)
        specs.append(anywhere)
    cells = count * ROWS * cols
    return pl.pallas_call(
        functools.partial(part_kernel, ROWS),
        grid=(count,),
        in_specs=specs,
        out_specs=pl.BlockSpec(block, lambda i: (PARTS * (first + i) + part, 0, 0)),
        out_shape=jax.ShapeDtypeStruct(pair_act.shape, jnp.bfloat16),
        input_output_aliases=aliases,
        cost_estimate=pl.CostEstimate(
            flops=cells * 196608 * 4, bytes_accessed=cells * 512, transcendentals=cells * 512
        ),
        compiler_params=pltpu.CompilerParams(vmem_limit_bytes=VMEM_BYTES),
        name="pair_part",
    )(*args)


def last_kernel(
    place_ref, pair_ref, done_ref, w_in_ref, w_out_ref, own_ref, other_ref, col_ref, out_ref,
    row_scr, col_scr,
):
    i = pl.program_id(0)
    cols = pair_ref.shape[1]

    @pl.when(i == 0)
    def _():
        row, col = place_ref[0], place_ref[1]
        for block in range(8):
            at = pl.ds(block * 16, 16)
            mine = pl.multiple_of((block ^ (col & 7)) * 16, 16)
            col_at = pl.multiple_of((block ^ row) * 16, 16)
            col_scr[at, :] = col_ref[pl.ds(col_at, 16), :].astype(jnp.float32)
            own_half = pl.multiple_of((col >> 3) * 128 + block * 16, 16)
            other_half = pl.multiple_of((1 - (col >> 3)) * 128 + block * 16, 16)
            row_scr[pl.ds(own_half, 16), :] = own_ref[pl.ds(mine, 16), :].astype(jnp.float32)
            row_scr[pl.ds(other_half, 16), :] = other_ref[pl.ds(mine, 16), :].astype(jnp.float32)

    size = PARTS * ROWS
    base = pl.multiple_of(i * size, size)
    col_add = col_scr[...]
    for r in range((PARTS - 1) * ROWS):
        extra = row_scr[pl.ds(base + r, 1), :] + col_add
        out_ref[r] = (done_ref[r].astype(jnp.float32) + extra).astype(jnp.bfloat16)
    step = SUB // cols
    for k in range(ROWS // step):
        cells = pair_ref[k * step : (k + 1) * step].reshape(SUB, 128)
        moved = transition(cells, w_in_ref[...], w_out_ref[...])
        for s in range(step):
            r = (PARTS - 1) * ROWS + k * step + s
            extra = row_scr[pl.ds(base + r, 1), :] + col_add
            out_ref[r] = (moved[s * cols : (s + 1) * cols] + extra).astype(jnp.bfloat16)


def last_part(place, pair_act, done, w_in, w_out, own, other, col):
    rows, cols, width = pair_act.shape
    count = rows // (PARTS * ROWS)
    big = (PARTS * ROWS, cols, width)
    whole = pl.BlockSpec(memory_space=pltpu.VMEM)
    return pl.pallas_call(
        last_kernel,
        grid=(count,),
        in_specs=[
            pl.BlockSpec(memory_space=pltpu.SMEM),
            pl.BlockSpec((ROWS, cols, width), lambda i: (PARTS * i + PARTS - 1, 0, 0)),
            pl.BlockSpec(big, lambda i: (i, 0, 0)),
            whole,
            whole,
            whole,
            whole,
            whole,
        ],
        out_specs=pl.BlockSpec(big, lambda i: (i, 0, 0)),
        out_shape=jax.ShapeDtypeStruct(pair_act.shape, jnp.bfloat16),
        scratch_shapes=[
            pltpu.VMEM((rows, width), jnp.float32),
            pltpu.VMEM((cols, width), jnp.float32),
        ],
        input_output_aliases={2: 0},
        cost_estimate=pl.CostEstimate(
            flops=rows * cols * 196608, bytes_accessed=rows * cols * 512, transcendentals=0
        ),
        compiler_params=pltpu.CompilerParams(vmem_limit_bytes=VMEM_BYTES),
        name="pair_last",
    )(place, pair_act, done, w_in, w_out, own, other, col)


def after(value, *others):
    return lax.optimization_barrier((value, *others))[0]


def on_device(
    pair_act, atom_act, atom_token, atom_gain, w_attn, w_out, w_bias, w_trans_in, w_trans_out,
    w_agg, w_single,
):
    atom_n, atom_width = atom_act.shape
    n_row, n_col = lax.axis_size("row"), lax.axis_size("col")
    devices = n_row * n_col
    row_index, col_index = lax.axis_index("row"), lax.axis_index("col")
    flat = row_index * n_col + col_index
    place = jnp.stack([row_index, col_index, flat, jnp.int32(devices * atom_n)]).astype(jnp.int32)
    both = ("row", "col")
    up = [(i, i + 1) for i in range(devices - 1)]
    down = [(i + 1, i) for i in range(devices - 1)]

    token_rel = (atom_token - flat * TOK_DEV).astype(jnp.bfloat16)
    tok_rows = jnp.broadcast_to(token_rel[None, :], (16, atom_n))
    below = lax.ppermute(jnp.concatenate([atom_act[-BELOW:], tok_rows]), both, up)
    above = lax.ppermute(jnp.concatenate([atom_act[:ABOVE], tok_rows]), both, down)

    width = w_trans_out.shape[0]
    scale = jnp.where(jnp.arange(2 * width) < width, 0.5, 1.0).astype(jnp.bfloat16)
    w_in = w_trans_in * scale[None, :]

    band = band_biases(place, pair_act, w_bias)
    near = lax.all_to_all(band, "col", 0, 0, tiled=True)
    moved = pair_part(pair_act, w_in, w_trans_out, 0, 0, 4, None, (band,))
    near, below, above = lax.optimization_barrier((near, below, above, moved))[:3]
    atom_out, next_out, token_single, singles = atom_part(
        place, below, atom_act, above, tok_rows, near, atom_gain[None, :], w_attn, w_out, w_agg,
        w_single,
    )

    held = singles
    from_below = lax.ppermute(next_out, both, up)
    for k in range(3):
        arrived = lax.ppermute(held, "col", [(i, i ^ (1 << k)) for i in range(n_col)])
        moved = pair_part(pair_act, w_in, w_trans_out, 1 + k // 2, 2 * (k % 2), 2, moved, (held,))
        arrived = after(arrived, moved)
        held = jnp.concatenate([held, arrived])
    row_own, col_own = held[:, :atom_width], held[:, atom_width:]
    row_other = lax.ppermute(row_own, "col", [(i, i ^ 8) for i in range(n_col)])
    turn = [(16 * a + 8 * h + k, 16 * k + 2 * a + h) for a in range(8) for h in range(2) for k in range(8)]
    col_tile = lax.ppermute(col_own, both, turn)
    moved = pair_part(pair_act, w_in, w_trans_out, 2, 2, 2, moved, (row_own, col_own))
    row_other, col_tile, from_below = lax.optimization_barrier(
        (row_other, col_tile, from_below, moved)
    )[:3]
    pair_out = last_part(
        place, pair_act, moved, w_in, w_trans_out, row_own, row_other, col_tile
    )
    shared = (atom_token < flat * TOK_DEV)[:16, None]
    atom_out = atom_out.at[:16].set(jnp.where(shared, from_below, atom_out[:16]))
    return (atom_out, token_single, pair_out)


def solution(mesh):
    both = P(("row", "col"), None)
    return jax.shard_map(
        on_device,
        mesh=mesh,
        in_specs=(P("row", "col", None), both, P(("row", "col"))) + (P(),) * 8,
        out_specs=(both, both, P("row", "col", None)),
        check_vma=False,
    )
```

```python
import functools
import math

import jax
import jax.numpy as jnp
from jax import lax
from jax.experimental import pallas as pl
from jax.experimental.pallas import tpu as pltpu
from jax.sharding import PartitionSpec as P

SPAN = 10
QB = 32
KW = 128
TOK_DEV = 16
BELOW = (KW - QB) // 2
ABOVE = KW - BELOW
WINDOW = 64
GROUPS = 9
BAND_ROWS = 32
EDGE = 48
BLOCK_ROWS = BAND_ROWS + 16 + ABOVE
BATCH = 3
VMEM_BYTES = 56 * 1024 * 1024
ROWS = 64
EARLY = 16
SUB = 512


def normalize(values):
    centre = values - jnp.mean(values, axis=-1, keepdims=True)
    spread = jnp.mean(centre * centre, axis=-1, keepdims=True)
    return centre * lax.rsqrt(spread + 1e-05)


def dot(a, b, **kw):
    return jnp.dot(a, b, preferred_element_type=jnp.float32, **kw)


def dot_nt(a, b):
    return lax.dot_general(a, b, (((1,), (1,)), ((), ())), preferred_element_type=jnp.float32)


def band_kernel(
    place_ref, pair_ref, weight_ref, atom_ref, token_ref, out_ref, cross_ref, tok_ref, cells, sems
):
    row, col = place_ref[0], place_ref[1]
    shift = col - 2 * row
    first = jnp.clip(8 * shift - 1, 0, 7)
    copies = []
    for j in range(GROUPS):
        group = first + j
        start = group - 8 * shift - 1
        begin = jnp.clip(start, 0, 4)
        at = jnp.clip(EDGE // 16 + begin - start, 0, 2 * EDGE // 16)
        copy = pltpu.make_async_copy(
            pair_ref.at[
                pl.ds(pl.multiple_of(group * 16, 16), 16),
                pl.ds(pl.multiple_of(begin * 16, 16), WINDOW),
                :,
            ],
            cells.at[j, :, pl.ds(pl.multiple_of(at * 16, 16), WINDOW), :],
            sems.at[j],
        )
        copy.start()
        copies.append(copy)
    out_ref[:, 0:BAND_ROWS, :] = jnp.zeros((out_ref.shape[0], BAND_ROWS, 128), jnp.bfloat16)
    atoms = atom_ref.shape[0]
    token_rel = (token_ref[...] - place_ref[2] * TOK_DEV).astype(jnp.float32)
    tok_rows = jnp.broadcast_to(token_rel, (16, 128)).astype(jnp.bfloat16)
    tok_ref[...] = tok_rows
    low = BAND_ROWS
    last = out_ref.shape[0] - 1

    def to_above(ref, at):
        ref[at : at + 16, :] = tok_rows
        ref[at + 16 : at + 16 + BELOW, :] = atom_ref[atoms - BELOW :, :]

    def to_below(ref, at):
        ref[at : at + 16, :] = tok_rows
        ref[at + 16 : at + 16 + ABOVE, :] = atom_ref[0:ABOVE, :]

    to_above(out_ref.at[jnp.minimum(col + 1, last)], low)
    to_below(out_ref.at[jnp.maximum(col - 1, 0)], low)

    @pl.when(col == last)
    def _():
        to_above(cross_ref, 0)
        to_below(out_ref.at[last - 1], low)

    @pl.when(col == 0)
    def _():
        to_below(cross_ref, 0)
        to_above(out_ref.at[1], low)

    weight = jnp.concatenate(
        [weight_ref[...].astype(jnp.float32), jnp.zeros((12, 128), jnp.float32)], axis=0
    ).astype(jnp.bfloat16)
    lane_piece = (lax.broadcasted_iota(jnp.int32, (BAND_ROWS, 128), 1) % WINDOW) // 16
    for j0 in range(0, GROUPS, BATCH):
        for j in range(j0, j0 + BATCH):
            copies[j].wait()
        flat = cells[j0 : j0 + BATCH, :, EDGE : EDGE + WINDOW, :].reshape(-1, 128)
        normed = normalize(flat.astype(jnp.float32)).astype(jnp.bfloat16)
        biases = dot_nt(weight, normed)
        for j in range(j0, j0 + BATCH):
            off = (j - j0) * 8
            rows = jnp.concatenate(
                [biases[0:4, 128 * (off + i) : 128 * (off + i + 1)] for i in range(8)], axis=0
            )
            at = first + j - 8 * shift - 1 + lane_piece
            kept = jnp.where((at >= 0) & (at <= 7), rows, 0.0)
            out_ref[pl.ds(first + j, 1), 0:BAND_ROWS, :] = kept.astype(jnp.bfloat16)[None]


def band_biases(place, pair_act, w_bias, atom_act, atom_token):
    vmem = pl.BlockSpec(memory_space=pltpu.VMEM)
    return pl.pallas_call(
        band_kernel,
        in_specs=[
            pl.BlockSpec(memory_space=pltpu.SMEM),
            pl.BlockSpec(memory_space=pl.ANY),
            vmem,
            vmem,
            vmem,
        ],
        out_specs=[vmem] * 3,
        out_shape=[
            jax.ShapeDtypeStruct((16, BLOCK_ROWS, 128), jnp.bfloat16),
            jax.ShapeDtypeStruct((16 + ABOVE, 128), jnp.bfloat16),
            jax.ShapeDtypeStruct((16, 128), jnp.bfloat16),
        ],
        scratch_shapes=[
            pltpu.VMEM((GROUPS, 16, WINDOW + 2 * EDGE, 128), jnp.bfloat16),
            pltpu.SemaphoreType.DMA((GROUPS,)),
        ],
        cost_estimate=pl.CostEstimate(flops=10**9, bytes_accessed=3 * 10**6, transcendentals=0),
        compiler_params=pltpu.CompilerParams(vmem_limit_bytes=VMEM_BYTES),
        name="band",
    )(place, pair_act, w_bias.T, atom_act, atom_token[None, :])


def atom_kernel(
    place_ref, cross_ref, own_ref, tok_ref, near_ref, gain_ref, wattn_ref, wout_ref,
    wagg_ref, wsingle_ref, atom_out_ref, next_out_ref, shared_ref, token_ref, singles_ref,
    wide, q_scr, k_scr, v_scr, gate_scr,
):
    flat = place_ref[2]
    atoms = own_ref.shape[0]
    heads = 4
    n_query = atoms + QB
    total = place_ref[3]
    col = place_ref[1]
    last = near_ref.shape[0] - 1
    low = BAND_ROWS
    from_below = near_ref[jnp.maximum(col - 1, 0), low : low + 16 + BELOW, :].astype(jnp.float32)
    from_above = near_ref[jnp.minimum(col + 1, last), low:, :].astype(jnp.float32)
    cross = cross_ref[...].astype(jnp.float32)
    from_below = jnp.where(col == 0, cross[0 : 16 + BELOW], from_below)
    from_above = jnp.where(col == last, cross, from_above)
    wide[0:BELOW, :] = from_below[16:]
    wide[BELOW : BELOW + atoms, :] = own_ref[...].astype(jnp.float32)
    wide[BELOW + atoms :, :] = from_above[16:]
    normed = (normalize(wide[...]) * gain_ref[...]).astype(jnp.bfloat16)
    projected = dot(normed, wattn_ref[...])
    q_scr[...] = projected[BELOW : BELOW + n_query, 0:128].astype(jnp.bfloat16)
    k_scr[...] = projected[:, 128:256].astype(jnp.bfloat16)
    v_scr[...] = projected[:, 256:384].astype(jnp.bfloat16)
    gate_scr[...] = jax.nn.sigmoid(projected[BELOW : BELOW + n_query, 384:512])

    tok_own = tok_ref[0:1, :].astype(jnp.float32)
    tok_below = from_below[0:1] - TOK_DEV
    tok_above = from_above[0:1] + TOK_DEV
    lane = lax.broadcasted_iota(jnp.int32, (8, 128), 1)
    rolled_own = pltpu.roll(jnp.broadcast_to(tok_own, (8, 128)), BELOW, 1)
    rolled_below = pltpu.roll(jnp.broadcast_to(tok_below, (8, 128)), BELOW, 1)
    rolled_above = pltpu.roll(jnp.broadcast_to(tok_above, (8, 128)), BELOW, 1)
    key_tok = jnp.concatenate(
        [
            jnp.where(lane < BELOW, rolled_below, rolled_own)[0:1],
            jnp.where(lane < BELOW, rolled_own, rolled_above)[0:1],
        ],
        axis=1,
    )
    col_own = jnp.transpose(jnp.broadcast_to(tok_own, (128, 128)))
    col_above = jnp.transpose(jnp.broadcast_to(tok_above, (128, 128)))

    band = jnp.sum(near_ref[:, 0:BAND_ROWS, :].astype(jnp.float32), axis=0)
    half = lax.broadcasted_iota(jnp.int32, (BAND_ROWS, 128), 1) < WINDOW
    band = jnp.concatenate([jnp.where(half, band, 0.0), jnp.where(half, 0.0, band)], axis=0)
    slot = (lax.broadcasted_iota(jnp.int32, (128, 256), 0) % WINDOW - 16).astype(jnp.float32)
    pick_key = (slot == key_tok).astype(jnp.bfloat16)
    spread = dot(band.astype(jnp.bfloat16), pick_key).astype(jnp.bfloat16)

    row_head = lax.broadcasted_iota(jnp.int32, (128, 128), 0) // QB
    lane_head = lax.broadcasted_iota(jnp.int32, (128, 128), 1) // 32
    own_head = row_head == lane_head
    entry = lax.broadcasted_iota(jnp.int32, (128, WINDOW), 1)
    entry_tok = (2 * ((entry % 32) // 4) + entry // 32).astype(jnp.float32)
    entry_head = entry % 4 == lax.broadcasted_iota(jnp.int32, (128, WINDOW), 0) // QB
    key_lane = lax.broadcasted_iota(jnp.int32, (128, KW), 1)
    for b in range(n_query // QB):
        at = b * QB
        queries = q_scr[at : at + QB, :]
        stacked = jnp.where(own_head, jnp.concatenate([queries] * heads, axis=0), 0)
        keys = k_scr[at : at + KW, :]
        tok_col = col_own[at : at + QB, 0:WINDOW] if at < atoms else col_above[0:QB, 0:WINDOW]
        pick = (jnp.concatenate([tok_col] * heads, axis=0) == entry_tok) & entry_head
        bias = dot(pick.astype(jnp.bfloat16), spread[:, at : at + KW])
        scores = dot_nt(stacked, keys) * (1.0 / math.sqrt(32)) + bias
        key_index = flat * atoms - BELOW + at + key_lane
        scores = jnp.where((key_index >= 0) & (key_index < total), scores, -jnp.inf)
        exponent = jnp.exp(scores - jnp.max(scores, axis=-1, keepdims=True))
        weights = (exponent / jnp.sum(exponent, axis=-1, keepdims=True)).astype(jnp.bfloat16)
        mixed = jnp.where(own_head, dot(weights, v_scr[at : at + KW, :]), 0.0)
        mixed = (mixed[0:32] + mixed[32:64]) + (mixed[64:96] + mixed[96:128])
        gate_scr[at : at + QB, :] = gate_scr[at : at + QB, :] * mixed
    attended = gate_scr[...].astype(jnp.bfloat16)
    atom_out = (wide[BELOW : BELOW + n_query, :] + dot(attended, wout_ref[...])).astype(
        jnp.bfloat16
    )
    atom_out_ref[...] = atom_out[0:atoms]
    next_out_ref[0:16, :] = atom_out[atoms : atoms + 16]
    next_out_ref[16:, :] = jnp.zeros((atoms - 16, 128), jnp.bfloat16)
    shared_ref[...] = col_own.astype(jnp.bfloat16)
    features = jnp.maximum(dot(atom_out, wagg_ref[...]), 0.0)
    tokens = lax.broadcasted_iota(jnp.int32, (TOK_DEV, 128), 0).astype(jnp.float32)
    member = (tok_own == tokens).astype(jnp.float32)
    member_next = ((tok_above == tokens) & (key_lane[0:TOK_DEV] < QB)).astype(jnp.float32)[:, 0:QB]
    counts = jnp.sum(member, axis=1, keepdims=True) + jnp.sum(member_next, axis=1, keepdims=True)
    totals = dot(member, features[0:atoms], precision=lax.Precision.HIGHEST) + dot(
        member_next, features[atoms:], precision=lax.Precision.HIGHEST
    )
    token_single = (totals / counts).astype(jnp.bfloat16)
    token_ref[...] = token_single
    singles = dot(token_single, wsingle_ref[...]).astype(jnp.bfloat16)
    singles_ref[...] = singles


def atom_part(place, cross, own, tok_rows, near, atom_gain, w_attn, w_out, w_agg, w_single):
    atoms = own.shape[0]
    vmem = pl.BlockSpec(memory_space=pltpu.VMEM)
    return pl.pallas_call(
        atom_kernel,
        in_specs=[pl.BlockSpec(memory_space=pltpu.SMEM)] + [vmem] * 9,
        out_specs=[vmem] * 5,
        out_shape=[
            jax.ShapeDtypeStruct((atoms, 128), jnp.bfloat16),
            jax.ShapeDtypeStruct((atoms, 128), jnp.bfloat16),
            jax.ShapeDtypeStruct((atoms, 128), jnp.bfloat16),
            jax.ShapeDtypeStruct((TOK_DEV, 384), jnp.bfloat16),
            jax.ShapeDtypeStruct((TOK_DEV, 256), jnp.bfloat16),
        ],
        scratch_shapes=[
            pltpu.VMEM((atoms + KW, 128), jnp.float32),
            pltpu.VMEM((atoms + QB, 128), jnp.bfloat16),
            pltpu.VMEM((atoms + KW, 128), jnp.bfloat16),
            pltpu.VMEM((atoms + KW, 128), jnp.bfloat16),
            pltpu.VMEM((atoms + QB, 128), jnp.float32),
        ],
        cost_estimate=pl.CostEstimate(flops=10**9, bytes_accessed=10**6, transcendentals=10**5),
        compiler_params=pltpu.CompilerParams(vmem_limit_bytes=VMEM_BYTES),
        name="atoms",
    )(place, cross, own, tok_rows, near, atom_gain, w_attn, w_out, w_agg, w_single)


def whole(array):
    return pl.BlockSpec(array.shape, lambda i: (0,) * array.ndim)


def halved_gate(w_in_ref, w_in_scr):
    width = w_in_ref.shape[1] // 2
    w_in_scr[:, :width] = w_in_ref[:, :width] * 0.5
    w_in_scr[:, width:] = w_in_ref[:, width:]


def transition(cells, w_in_scr, w_out_ref):
    width = w_out_ref.shape[0]
    wide = cells.reshape(-1, 128).astype(jnp.float32)
    hidden = dot(normalize(wide).astype(jnp.bfloat16), w_in_scr[...])
    gate = hidden[:, :width].astype(jnp.bfloat16)
    up = hidden[:, width:].astype(jnp.bfloat16)
    return wide + dot((gate + gate * jnp.tanh(gate)) * up, w_out_ref[...])


def early_kernel(pair_ref, w_in_ref, w_out_ref, band_ref, out_ref, w_in_scr):
    rows, cols, _ = pair_ref.shape

    @pl.when(pl.program_id(0) == 0)
    def _():
        halved_gate(w_in_ref, w_in_scr)

    step = SUB // cols
    for k in range(0, rows, step):
        moved = transition(pair_ref[k : k + step], w_in_scr, w_out_ref)
        out_ref[k : k + step] = moved.astype(jnp.bfloat16).reshape(step, cols, 128)


def early_part(pair_act, w_in, w_out, band):
    rows, cols, width = pair_act.shape
    block = pl.BlockSpec((EARLY, cols, width), lambda i: (ROWS // EARLY * i, 0, 0))
    cells = rows // ROWS * EARLY * cols
    return pl.pallas_call(
        early_kernel,
        grid=(rows // ROWS,),
        in_specs=[block, whole(w_in), whole(w_out), pl.BlockSpec(memory_space=pl.ANY)],
        out_specs=block,
        out_shape=jax.ShapeDtypeStruct(pair_act.shape, jnp.bfloat16),
        scratch_shapes=[pltpu.VMEM(w_in.shape, jnp.bfloat16)],
        cost_estimate=pl.CostEstimate(
            flops=cells * 196608 * 2, bytes_accessed=cells * 512, transcendentals=0
        ),
        compiler_params=pltpu.CompilerParams(vmem_limit_bytes=VMEM_BYTES),
        name="pair_early",
    )(pair_act, w_in, w_out, band)


def last_kernel(
    place_ref, pair_ref, done_ref, w_in_ref, w_out_ref, own_ref, other_ref, col_ref,
    out_ref, w_in_scr, row_scr, col_scr,
):
    i = pl.program_id(0)
    rows, cols, _ = pair_ref.shape

    @pl.when(i == 0)
    def _():
        halved_gate(w_in_ref, w_in_scr)
        row, col = place_ref[0], place_ref[1]
        half = col // 8
        for block in range(8):
            at = slice(block * TOK_DEV, (block + 1) * TOK_DEV)
            row_at = pl.ds(pl.multiple_of((block ^ (col % 8)) * 16, 16), 16)
            col_at = pl.ds(pl.multiple_of((block ^ row) * 16, 16), 16)
            own_to = pl.ds(pl.multiple_of(half * 128 + block * 16, 16), 16)
            other_to = pl.ds(pl.multiple_of((1 - half) * 128 + block * 16, 16), 16)
            row_scr[own_to, :] = own_ref[row_at, 0:128].astype(jnp.float32)
            row_scr[other_to, :] = other_ref[row_at, 0:128].astype(jnp.float32)
            col_scr[at, :] = col_ref[col_at, 128:256].astype(jnp.float32)

    base = pl.multiple_of(i * rows, rows)
    col_add = col_scr[...]
    step = SUB // cols
    for k in range(EARLY, rows, step):
        moved = transition(pair_ref[k : k + step], w_in_scr, w_out_ref)
        for s in range(step):
            extra = row_scr[pl.ds(base + k + s, 1), :] + col_add
            out_ref[k + s] = (moved[s * cols : (s + 1) * cols] + extra).astype(jnp.bfloat16)
    for r in range(EARLY):
        extra = row_scr[pl.ds(base + r, 1), :] + col_add
        out_ref[r] = (done_ref[r].astype(jnp.float32) + extra).astype(jnp.bfloat16)


def last_part(place, pair_act, done, w_in, w_out, own, other, col):
    rows, cols, width = pair_act.shape
    block = pl.BlockSpec((ROWS, cols, width), lambda i: (i, 0, 0))
    done_block = pl.BlockSpec((EARLY, cols, width), lambda i: (ROWS // EARLY * i, 0, 0))
    return pl.pallas_call(
        last_kernel,
        grid=(rows // ROWS,),
        in_specs=[pl.BlockSpec(memory_space=pltpu.SMEM), block, done_block]
        + [whole(x) for x in (w_in, w_out, own, other, col)],
        out_specs=block,
        out_shape=jax.ShapeDtypeStruct(pair_act.shape, jnp.bfloat16),
        scratch_shapes=[
            pltpu.VMEM(w_in.shape, jnp.bfloat16),
            pltpu.VMEM((rows, width), jnp.float32),
            pltpu.VMEM((cols, width), jnp.float32),
        ],
        cost_estimate=pl.CostEstimate(
            flops=rows * cols * 196608 * 2, bytes_accessed=rows * cols * 512, transcendentals=0
        ),
        compiler_params=pltpu.CompilerParams(vmem_limit_bytes=VMEM_BYTES),
        name="pair_last",
    )(place, pair_act, done, w_in, w_out, own, other, col)


def on_device(
    pair_act, atom_act, atom_token, atom_gain, w_attn, w_out, w_bias, w_trans_in, w_trans_out,
    w_agg, w_single,
):
    atom_n = atom_act.shape[0]
    n_row, n_col = lax.axis_size("row"), lax.axis_size("col")
    devices = n_row * n_col
    row_index, col_index = lax.axis_index("row"), lax.axis_index("col")
    flat = row_index * n_col + col_index
    place = jnp.stack([row_index, col_index, flat, jnp.int32(devices * atom_n)]).astype(jnp.int32)
    both = ("row", "col")
    up = [(i, i + 1) for i in range(devices - 1)]
    firsts = [n_col * i for i in range(1, n_row)]
    ends = [(i - 1, i) for i in firsts] + [(i, i - 1) for i in firsts]
    turn = [
        (16 * a + 8 * h + k, 16 * k + 2 * a + h)
        for a in range(n_row)
        for h in range(2)
        for k in range(8)
    ]

    band, cross, tok_rows = band_biases(place, pair_act, w_bias, atom_act, atom_token)
    cross = lax.ppermute(cross, both, ends)
    near = lax.all_to_all(band, "col", 0, 0, tiled=True)
    done = early_part(pair_act, w_trans_in, w_trans_out, band)
    near, cross = lax.optimization_barrier((near, cross, done))[:2]
    atom_main, next_out, shared, token_single, singles = atom_part(
        place, cross, atom_act, tok_rows, near, atom_gain[None, :], w_attn, w_out, w_agg, w_single
    )
    held = singles
    for k in range(3):
        pairs = [(i, i ^ (1 << k)) for i in range(n_col)]
        held = jnp.concatenate([held, lax.ppermute(held, "col", pairs)])
    col_all = lax.ppermute(held, both, turn)
    other = lax.ppermute(held, "col", [(i, i ^ 8) for i in range(n_col)])
    from_below = lax.ppermute(next_out, both, up)
    pair_out = last_part(
        place, pair_act, done, w_trans_in, w_trans_out, held, other, col_all
    )
    from_below = lax.optimization_barrier((from_below, pair_out))[0]
    atom_out = jnp.where(shared < 0, from_below, atom_main)
    return (atom_out, token_single, pair_out)


def solution(mesh):
    both = P(("row", "col"), None)
    return jax.shard_map(
        on_device,
        mesh=mesh,
        in_specs=(P("row", "col", None), both, P(("row", "col"))) + (P(),) * 8,
        out_specs=(both, both, P("row", "col", None)),
        check_vma=False,
    )
```

```python
import functools
import math

import jax
import jax.numpy as jnp
from jax import lax
from jax.experimental import pallas as pl
from jax.experimental.pallas import tpu as pltpu
from jax.sharding import PartitionSpec as P

SPAN = 10
QB = 32
KW = 128
TOK_DEV = 16
BELOW = (KW - QB) // 2
ABOVE = KW - BELOW
WINDOW = 64
GROUPS = 9
BAND_ROWS = 32
EDGE = 48
BLOCK_ROWS = BAND_ROWS + 16 + ABOVE
BATCH = 3
MIB = 1024 * 1024
WIDE = 50
ROWS = 64
EARLY = 16
SUB = 512


def normalize(values):
    centre = values - jnp.mean(values, axis=-1, keepdims=True)
    spread = jnp.mean(centre * centre, axis=-1, keepdims=True)
    return centre * lax.rsqrt(spread + 1e-05)


def dot(a, b, **kw):
    return jnp.dot(a, b, preferred_element_type=jnp.float32, **kw)


def dot_nt(a, b):
    return lax.dot_general(a, b, (((1,), (1,)), ((), ())), preferred_element_type=jnp.float32)


def band_kernel(
    place_ref, pair_ref, weight_ref, atom_ref, token_ref, out_ref, cross_ref, tok_ref, cells, sems
):
    row, col = place_ref[0], place_ref[1]
    shift = col - 2 * row
    first = jnp.clip(8 * shift - 1, 0, 7)
    copies = []
    for j in range(GROUPS):
        group = first + j
        start = group - 8 * shift - 1
        begin = jnp.clip(start, 0, 4)
        at = jnp.clip(EDGE // 16 + begin - start, 0, 2 * EDGE // 16)
        copy = pltpu.make_async_copy(
            pair_ref.at[
                pl.ds(pl.multiple_of(group * 16, 16), 16),
                pl.ds(pl.multiple_of(begin * 16, 16), WINDOW),
                :,
            ],
            cells.at[j, :, pl.ds(pl.multiple_of(at * 16, 16), WINDOW), :],
            sems.at[j],
        )
        copy.start()
        copies.append(copy)
    out_ref[:, 0:BAND_ROWS, :] = jnp.zeros((out_ref.shape[0], BAND_ROWS, 128), jnp.bfloat16)
    atoms = atom_ref.shape[0]
    token_rel = (token_ref[...] - place_ref[2] * TOK_DEV).astype(jnp.float32)
    tok_rows = jnp.broadcast_to(token_rel, (16, 128)).astype(jnp.bfloat16)
    tok_ref[...] = tok_rows
    low = BAND_ROWS
    last = out_ref.shape[0] - 1

    def to_above(ref, at):
        ref[at : at + 16, :] = tok_rows
        ref[at + 16 : at + 16 + BELOW, :] = atom_ref[atoms - BELOW :, :]

    def to_below(ref, at):
        ref[at : at + 16, :] = tok_rows
        ref[at + 16 : at + 16 + ABOVE, :] = atom_ref[0:ABOVE, :]

    to_above(out_ref.at[jnp.minimum(col + 1, last)], low)
    to_below(out_ref.at[jnp.maximum(col - 1, 0)], low)

    @pl.when(col == last)
    def _():
        to_above(cross_ref, 0)
        to_below(out_ref.at[last - 1], low)

    @pl.when(col == 0)
    def _():
        to_below(cross_ref, 0)
        to_above(out_ref.at[1], low)

    weight = jnp.concatenate(
        [weight_ref[...].astype(jnp.float32), jnp.zeros((12, 128), jnp.float32)], axis=0
    ).astype(jnp.bfloat16)
    lane_piece = (lax.broadcasted_iota(jnp.int32, (BAND_ROWS, 128), 1) % WINDOW) // 16
    for j0 in range(0, GROUPS, BATCH):
        for j in range(j0, j0 + BATCH):
            copies[j].wait()
        flat = cells[j0 : j0 + BATCH, :, EDGE : EDGE + WINDOW, :].reshape(-1, 128)
        normed = normalize(flat.astype(jnp.float32)).astype(jnp.bfloat16)
        biases = dot_nt(weight, normed)
        for j in range(j0, j0 + BATCH):
            off = (j - j0) * 8
            rows = jnp.concatenate(
                [biases[0:4, 128 * (off + i) : 128 * (off + i + 1)] for i in range(8)], axis=0
            )
            at = first + j - 8 * shift - 1 + lane_piece
            kept = jnp.where((at >= 0) & (at <= 7), rows, 0.0)
            out_ref[pl.ds(first + j, 1), 0:BAND_ROWS, :] = kept.astype(jnp.bfloat16)[None]


def band_biases(place, pair_act, w_bias, atom_act, atom_token):
    vmem = pl.BlockSpec(memory_space=pltpu.VMEM)
    return pl.pallas_call(
        band_kernel,
        in_specs=[
            pl.BlockSpec(memory_space=pltpu.SMEM),
            pl.BlockSpec(memory_space=pl.ANY),
            vmem,
            vmem,
            vmem,
        ],
        out_specs=[vmem] * 3,
        out_shape=[
            jax.ShapeDtypeStruct((16, BLOCK_ROWS, 128), jnp.bfloat16),
            jax.ShapeDtypeStruct((16 + ABOVE, 128), jnp.bfloat16),
            jax.ShapeDtypeStruct((16, 128), jnp.bfloat16),
        ],
        scratch_shapes=[
            pltpu.VMEM((GROUPS, 16, WINDOW + 2 * EDGE, 128), jnp.bfloat16),
            pltpu.SemaphoreType.DMA((GROUPS,)),
        ],
        cost_estimate=pl.CostEstimate(flops=10**9, bytes_accessed=3 * 10**6, transcendentals=0),
        compiler_params=pltpu.CompilerParams(vmem_limit_bytes=56 * MIB),
        name="band",
    )(place, pair_act, w_bias.T, atom_act, atom_token[None, :])


def atom_kernel(
    place_ref, cross_ref, own_ref, tok_ref, near_ref, gain_ref, wattn_ref, wout_ref,
    wagg_ref, wsingle_ref, atom_out_ref, next_out_ref, shared_ref, token_ref, singles_ref,
    wide, q_scr, k_scr, v_scr, gate_scr,
):
    flat = place_ref[2]
    atoms = own_ref.shape[0]
    heads = 4
    n_query = atoms + QB
    total = place_ref[3]
    col = place_ref[1]
    last = near_ref.shape[0] - 1
    low = BAND_ROWS
    from_below = near_ref[jnp.maximum(col - 1, 0), low : low + 16 + BELOW, :].astype(jnp.float32)
    from_above = near_ref[jnp.minimum(col + 1, last), low:, :].astype(jnp.float32)
    cross = cross_ref[...].astype(jnp.float32)
    from_below = jnp.where(col == 0, cross[0 : 16 + BELOW], from_below)
    from_above = jnp.where(col == last, cross, from_above)
    wide[0:BELOW, :] = from_below[16:]
    wide[BELOW : BELOW + atoms, :] = own_ref[...].astype(jnp.float32)
    wide[BELOW + atoms :, :] = from_above[16:]
    normed = (normalize(wide[...]) * gain_ref[...]).astype(jnp.bfloat16)
    projected = dot(normed, wattn_ref[...])
    q_scr[...] = projected[BELOW : BELOW + n_query, 0:128].astype(jnp.bfloat16)
    k_scr[...] = projected[:, 128:256].astype(jnp.bfloat16)
    v_scr[...] = projected[:, 256:384].astype(jnp.bfloat16)
    gate_scr[...] = jax.nn.sigmoid(projected[BELOW : BELOW + n_query, 384:512])

    tok_own = tok_ref[0:1, :].astype(jnp.float32)
    tok_below = from_below[0:1] - TOK_DEV
    tok_above = from_above[0:1] + TOK_DEV
    lane = lax.broadcasted_iota(jnp.int32, (8, 128), 1)
    rolled_own = pltpu.roll(jnp.broadcast_to(tok_own, (8, 128)), BELOW, 1)
    rolled_below = pltpu.roll(jnp.broadcast_to(tok_below, (8, 128)), BELOW, 1)
    rolled_above = pltpu.roll(jnp.broadcast_to(tok_above, (8, 128)), BELOW, 1)
    key_tok = jnp.concatenate(
        [
            jnp.where(lane < BELOW, rolled_below, rolled_own)[0:1],
            jnp.where(lane < BELOW, rolled_own, rolled_above)[0:1],
        ],
        axis=1,
    )
    col_own = jnp.transpose(jnp.broadcast_to(tok_own, (128, 128)))
    col_above = jnp.transpose(jnp.broadcast_to(tok_above, (128, 128)))

    band = jnp.sum(near_ref[:, 0:BAND_ROWS, :].astype(jnp.float32), axis=0)
    half = lax.broadcasted_iota(jnp.int32, (BAND_ROWS, 128), 1) < WINDOW
    band = jnp.concatenate([jnp.where(half, band, 0.0), jnp.where(half, 0.0, band)], axis=0)
    slot = (lax.broadcasted_iota(jnp.int32, (128, 256), 0) % WINDOW - 16).astype(jnp.float32)
    pick_key = (slot == key_tok).astype(jnp.bfloat16)
    spread = dot(band.astype(jnp.bfloat16), pick_key).astype(jnp.bfloat16)

    row_head = lax.broadcasted_iota(jnp.int32, (128, 128), 0) // QB
    lane_head = lax.broadcasted_iota(jnp.int32, (128, 128), 1) // 32
    own_head = row_head == lane_head
    entry = lax.broadcasted_iota(jnp.int32, (128, WINDOW), 1)
    entry_tok = (2 * ((entry % 32) // 4) + entry // 32).astype(jnp.float32)
    entry_head = entry % 4 == lax.broadcasted_iota(jnp.int32, (128, WINDOW), 0) // QB
    key_lane = lax.broadcasted_iota(jnp.int32, (128, KW), 1)
    for b in range(n_query // QB):
        at = b * QB
        queries = q_scr[at : at + QB, :]
        stacked = jnp.where(own_head, jnp.concatenate([queries] * heads, axis=0), 0)
        keys = k_scr[at : at + KW, :]
        tok_col = col_own[at : at + QB, 0:WINDOW] if at < atoms else col_above[0:QB, 0:WINDOW]
        pick = (jnp.concatenate([tok_col] * heads, axis=0) == entry_tok) & entry_head
        bias = dot(pick.astype(jnp.bfloat16), spread[:, at : at + KW])
        scores = dot_nt(stacked, keys) * (1.0 / math.sqrt(32)) + bias
        key_index = flat * atoms - BELOW + at + key_lane
        scores = jnp.where((key_index >= 0) & (key_index < total), scores, -jnp.inf)
        exponent = jnp.exp(scores - jnp.max(scores, axis=-1, keepdims=True))
        weights = (exponent / jnp.sum(exponent, axis=-1, keepdims=True)).astype(jnp.bfloat16)
        mixed = jnp.where(own_head, dot(weights, v_scr[at : at + KW, :]), 0.0)
        mixed = (mixed[0:32] + mixed[32:64]) + (mixed[64:96] + mixed[96:128])
        gate_scr[at : at + QB, :] = gate_scr[at : at + QB, :] * mixed
    attended = gate_scr[...].astype(jnp.bfloat16)
    atom_out = (wide[BELOW : BELOW + n_query, :] + dot(attended, wout_ref[...])).astype(
        jnp.bfloat16
    )
    atom_out_ref[...] = atom_out[0:atoms]
    next_out_ref[0:16, :] = atom_out[atoms : atoms + 16]
    next_out_ref[16:, :] = jnp.zeros((atoms - 16, 128), jnp.bfloat16)
    shared_ref[...] = col_own.astype(jnp.bfloat16)
    features = jnp.maximum(dot(atom_out, wagg_ref[...]), 0.0)
    tokens = lax.broadcasted_iota(jnp.int32, (TOK_DEV, 128), 0).astype(jnp.float32)
    member = (tok_own == tokens).astype(jnp.float32)
    member_next = ((tok_above == tokens) & (key_lane[0:TOK_DEV] < QB)).astype(jnp.float32)[:, 0:QB]
    counts = jnp.sum(member, axis=1, keepdims=True) + jnp.sum(member_next, axis=1, keepdims=True)
    totals = dot(member, features[0:atoms], precision=lax.Precision.HIGHEST) + dot(
        member_next, features[atoms:], precision=lax.Precision.HIGHEST
    )
    token_single = (totals / counts).astype(jnp.bfloat16)
    token_ref[...] = token_single
    singles = dot(token_single, wsingle_ref[...]).astype(jnp.bfloat16)
    singles_ref[...] = singles


def atom_part(place, cross, own, tok_rows, near, atom_gain, w_attn, w_out, w_agg, w_single):
    atoms = own.shape[0]
    vmem = pl.BlockSpec(memory_space=pltpu.VMEM)
    return pl.pallas_call(
        atom_kernel,
        in_specs=[pl.BlockSpec(memory_space=pltpu.SMEM)] + [vmem] * 9,
        out_specs=[vmem] * 5,
        out_shape=[
            jax.ShapeDtypeStruct((atoms, 128), jnp.bfloat16),
            jax.ShapeDtypeStruct((atoms, 128), jnp.bfloat16),
            jax.ShapeDtypeStruct((atoms, 128), jnp.bfloat16),
            jax.ShapeDtypeStruct((TOK_DEV, 384), jnp.bfloat16),
            jax.ShapeDtypeStruct((TOK_DEV, 256), jnp.bfloat16),
        ],
        scratch_shapes=[
            pltpu.VMEM((atoms + KW, 128), jnp.float32),
            pltpu.VMEM((atoms + QB, 128), jnp.bfloat16),
            pltpu.VMEM((atoms + KW, 128), jnp.bfloat16),
            pltpu.VMEM((atoms + KW, 128), jnp.bfloat16),
            pltpu.VMEM((atoms + QB, 128), jnp.float32),
        ],
        cost_estimate=pl.CostEstimate(flops=10**9, bytes_accessed=10**6, transcendentals=10**5),
        compiler_params=pltpu.CompilerParams(vmem_limit_bytes=16 * MIB),
        name="atoms",
    )(place, cross, own, tok_rows, near, atom_gain, w_attn, w_out, w_agg, w_single)


def whole(array):
    return pl.BlockSpec(array.shape, lambda i: (0,) * array.ndim)


def halved_gate(w_in_ref, w_in_scr):
    width = w_in_ref.shape[1] // 2
    w_in_scr[:, :width] = w_in_ref[:, :width] * 0.5
    w_in_scr[:, width:] = w_in_ref[:, width:]


def transition(cells, w_in_scr, w_out_ref):
    width = w_out_ref.shape[0]
    wide = cells.reshape(-1, 128).astype(jnp.float32)
    hidden = dot(normalize(wide).astype(jnp.bfloat16), w_in_scr[...])
    gate = hidden[:, :width].astype(jnp.bfloat16)
    up = hidden[:, width:].astype(jnp.bfloat16)
    return wide + dot((gate + gate * jnp.tanh(gate)) * up, w_out_ref[...])


def early_kernel(pair_ref, w_in_ref, w_out_ref, band_ref, out_ref, w_in_scr):
    rows, cols, _ = pair_ref.shape

    @pl.when(pl.program_id(0) == 0)
    def _():
        halved_gate(w_in_ref, w_in_scr)

    step = SUB // cols
    for k in range(0, rows, step):
        moved = transition(pair_ref[k : k + step], w_in_scr, w_out_ref)
        out_ref[k : k + step] = moved.astype(jnp.bfloat16).reshape(step, cols, 128)


def early_part(pair_act, w_in, w_out, band):
    rows, cols, width = pair_act.shape
    block = pl.BlockSpec((EARLY, cols, width), lambda i: (ROWS // EARLY * i, 0, 0))
    cells = rows // ROWS * EARLY * cols
    return pl.pallas_call(
        early_kernel,
        grid=(rows // ROWS,),
        in_specs=[block, whole(w_in), whole(w_out), pl.BlockSpec(memory_space=pl.ANY)],
        out_specs=block,
        out_shape=jax.ShapeDtypeStruct(pair_act.shape, jnp.bfloat16),
        scratch_shapes=[pltpu.VMEM(w_in.shape, jnp.bfloat16)],
        cost_estimate=pl.CostEstimate(
            flops=cells * 196608 * 2, bytes_accessed=cells * 512, transcendentals=0
        ),
        compiler_params=pltpu.CompilerParams(vmem_limit_bytes=WIDE * MIB),
        name="pair_early",
    )(pair_act, w_in, w_out, band)


def last_kernel(
    place_ref, pair_ref, done_ref, w_in_ref, w_out_ref, own_ref, other_ref, col_ref,
    out_ref, w_in_scr, row_scr, col_scr,
):
    i = pl.program_id(0)
    rows, cols, _ = pair_ref.shape

    @pl.when(i == 0)
    def _():
        halved_gate(w_in_ref, w_in_scr)
        row, col = place_ref[0], place_ref[1]
        half = col // 8
        for block in range(8):
            at = slice(block * TOK_DEV, (block + 1) * TOK_DEV)
            row_at = pl.ds(pl.multiple_of((block ^ (col % 8)) * 16, 16), 16)
            col_at = pl.ds(pl.multiple_of((block ^ row) * 16, 16), 16)
            own_to = pl.ds(pl.multiple_of(half * 128 + block * 16, 16), 16)
            other_to = pl.ds(pl.multiple_of((1 - half) * 128 + block * 16, 16), 16)
            row_scr[own_to, :] = own_ref[row_at, 0:128].astype(jnp.float32)
            row_scr[other_to, :] = other_ref[row_at, 0:128].astype(jnp.float32)
            col_scr[at, :] = col_ref[col_at, 128:256].astype(jnp.float32)

    base = pl.multiple_of(i * rows, rows)
    col_add = col_scr[...]
    step = SUB // cols
    for k in range(EARLY, rows, step):
        moved = transition(pair_ref[k : k + step], w_in_scr, w_out_ref)
        for s in range(step):
            extra = row_scr[pl.ds(base + k + s, 1), :] + col_add
            out_ref[k + s] = (moved[s * cols : (s + 1) * cols] + extra).astype(jnp.bfloat16)
    for r in range(EARLY):
        extra = row_scr[pl.ds(base + r, 1), :] + col_add
        out_ref[r] = (done_ref[r].astype(jnp.float32) + extra).astype(jnp.bfloat16)


def last_part(place, pair_act, done, w_in, w_out, own, other, col):
    rows, cols, width = pair_act.shape
    block = pl.BlockSpec((ROWS, cols, width), lambda i: (i, 0, 0))
    done_block = pl.BlockSpec((EARLY, cols, width), lambda i: (ROWS // EARLY * i, 0, 0))
    return pl.pallas_call(
        last_kernel,
        grid=(rows // ROWS,),
        in_specs=[pl.BlockSpec(memory_space=pltpu.SMEM), block, done_block]
        + [whole(x) for x in (w_in, w_out, own, other, col)],
        out_specs=block,
        out_shape=jax.ShapeDtypeStruct(pair_act.shape, jnp.bfloat16),
        scratch_shapes=[
            pltpu.VMEM(w_in.shape, jnp.bfloat16),
            pltpu.VMEM((rows, width), jnp.float32),
            pltpu.VMEM((cols, width), jnp.float32),
        ],
        cost_estimate=pl.CostEstimate(
            flops=rows * cols * 196608 * 2, bytes_accessed=rows * cols * 512, transcendentals=0
        ),
        compiler_params=pltpu.CompilerParams(vmem_limit_bytes=WIDE * MIB),
        name="pair_last",
    )(place, pair_act, done, w_in, w_out, own, other, col)


def on_device(
    pair_act, atom_act, atom_token, atom_gain, w_attn, w_out, w_bias, w_trans_in, w_trans_out,
    w_agg, w_single,
):
    atom_n = atom_act.shape[0]
    n_row, n_col = lax.axis_size("row"), lax.axis_size("col")
    devices = n_row * n_col
    row_index, col_index = lax.axis_index("row"), lax.axis_index("col")
    flat = row_index * n_col + col_index
    place = jnp.stack([row_index, col_index, flat, jnp.int32(devices * atom_n)]).astype(jnp.int32)
    both = ("row", "col")
    up = [(i, i + 1) for i in range(devices - 1)]
    firsts = [n_col * i for i in range(1, n_row)]
    ends = [(i - 1, i) for i in firsts] + [(i, i - 1) for i in firsts]
    turn = [
        (16 * a + 8 * h + k, 16 * k + 2 * a + h)
        for a in range(n_row)
        for h in range(2)
        for k in range(8)
    ]

    band, cross, tok_rows = band_biases(place, pair_act, w_bias, atom_act, atom_token)
    cross = lax.ppermute(cross, both, ends)
    near = lax.all_to_all(band, "col", 0, 0, tiled=True)
    done = early_part(pair_act, w_trans_in, w_trans_out, band)
    near, cross = lax.optimization_barrier((near, cross, done))[:2]
    atom_main, next_out, shared, token_single, singles = atom_part(
        place, cross, atom_act, tok_rows, near, atom_gain[None, :], w_attn, w_out, w_agg, w_single
    )
    held = singles
    for k in range(3):
        pairs = [(i, i ^ (1 << k)) for i in range(n_col)]
        held = jnp.concatenate([held, lax.ppermute(held, "col", pairs)])
    col_all = lax.ppermute(held, both, turn)
    other = lax.ppermute(held, "col", [(i, i ^ 8) for i in range(n_col)])
    from_below = lax.ppermute(next_out, both, up)
    pair_out = last_part(
        place, pair_act, done, w_trans_in, w_trans_out, held, other, col_all
    )
    from_below = lax.optimization_barrier((from_below, pair_out))[0]
    atom_out = jnp.where(shared < 0, from_below, atom_main)
    return (atom_out, token_single, pair_out)


def solution(mesh):
    both = P(("row", "col"), None)
    return jax.shard_map(
        on_device,
        mesh=mesh,
        in_specs=(P("row", "col", None), both, P(("row", "col"))) + (P(),) * 8,
        out_specs=(both, both, P("row", "col", None)),
        check_vma=False,
    )
```

```python
import functools
import math

import jax
import jax.numpy as jnp
import numpy as np
from jax import lax
from jax.experimental import pallas as pl
from jax.experimental.pallas import tpu as pltpu
from jax.sharding import PartitionSpec as P

SPAN = 10
QB = 32
KW = 128
TOK_DEV = 16
BELOW = (KW - QB) // 2
ABOVE = KW - BELOW
WINDOW = 64
GROUPS = 9
BAND_ROWS = 32
EDGE = 48
BLOCK_ROWS = BAND_ROWS + 16 + ABOVE
BATCH = 3
MIB = 1024 * 1024
WIDE = 50
ROWS = 64
EARLY = 16
SUB = 512


def normalize(values):
    centre = values - jnp.mean(values, axis=-1, keepdims=True)
    spread = jnp.mean(centre * centre, axis=-1, keepdims=True)
    return centre * lax.rsqrt(spread + 1e-05)


def dot(a, b, **kw):
    return jnp.dot(a, b, preferred_element_type=jnp.float32, **kw)


def dot_nt(a, b):
    return lax.dot_general(a, b, (((1,), (1,)), ((), ())), preferred_element_type=jnp.float32)


def band_kernel(
    place_ref, pair_ref, weight_ref, atom_ref, token_ref, far_atom_ref, far_token_ref, out_ref,
    tok_ref, cells, sems,
):
    row, col = place_ref[0], place_ref[1]
    shift = col - 2 * row
    first = jnp.clip(8 * shift - 1, 0, 7)
    copies = []
    for j in range(GROUPS):
        group = first + j
        start = group - 8 * shift - 1
        begin = jnp.clip(start, 0, 4)
        at = jnp.clip(EDGE // 16 + begin - start, 0, 2 * EDGE // 16)
        copy = pltpu.make_async_copy(
            pair_ref.at[
                pl.ds(pl.multiple_of(group * 16, 16), 16),
                pl.ds(pl.multiple_of(begin * 16, 16), WINDOW),
                :,
            ],
            cells.at[j, :, pl.ds(pl.multiple_of(at * 16, 16), WINDOW), :],
            sems.at[j],
        )
        copy.start()
        copies.append(copy)
    out_ref[:, 0:BAND_ROWS, :] = jnp.zeros((out_ref.shape[0], BAND_ROWS, 128), jnp.bfloat16)
    atoms = atom_ref.shape[0]
    token_rel = (token_ref[...] - place_ref[2] * TOK_DEV).astype(jnp.float32)
    tok_rows = jnp.broadcast_to(token_rel, (16, 128)).astype(jnp.bfloat16)
    tok_ref[...] = tok_rows
    low = BAND_ROWS
    last = out_ref.shape[0] - 1

    def to_above(ref, rows, source):
        ref[low : low + 16, :] = rows
        ref[low + 16 : low + 16 + BELOW, :] = source[atoms - BELOW :, :]

    def to_below(ref, rows, source):
        ref[low : low + 16, :] = rows
        ref[low + 16 : low + 16 + ABOVE, :] = source[0:ABOVE, :]

    @pl.when(col < last)
    def _():
        to_above(out_ref.at[col + 1], tok_rows, atom_ref)

    @pl.when(col > 0)
    def _():
        to_below(out_ref.at[col - 1], tok_rows, atom_ref)

    def far_rows(first_token):
        far = (far_token_ref[...] - first_token).astype(jnp.float32)
        return jnp.broadcast_to(far, (16, 128)).astype(jnp.bfloat16)

    wide_row = TOK_DEV * (last + 1)

    @pl.when(col == last)
    def _():
        to_above(out_ref.at[0], far_rows(place_ref[2] * TOK_DEV - wide_row), far_atom_ref)

    @pl.when(col == 0)
    def _():
        to_below(out_ref.at[last], far_rows(place_ref[2] * TOK_DEV + wide_row), far_atom_ref)

    weight = jnp.concatenate(
        [weight_ref[...].astype(jnp.float32), jnp.zeros((12, 128), jnp.float32)], axis=0
    ).astype(jnp.bfloat16)
    lane_piece = (lax.broadcasted_iota(jnp.int32, (BAND_ROWS, 128), 1) % WINDOW) // 16
    for j0 in range(0, GROUPS, BATCH):
        for j in range(j0, j0 + BATCH):
            copies[j].wait()
        flat = cells[j0 : j0 + BATCH, :, EDGE : EDGE + WINDOW, :].reshape(-1, 128)
        normed = normalize(flat.astype(jnp.float32)).astype(jnp.bfloat16)
        biases = dot_nt(weight, normed)
        for j in range(j0, j0 + BATCH):
            off = (j - j0) * 8
            rows = jnp.concatenate(
                [biases[0:4, 128 * (off + i) : 128 * (off + i + 1)] for i in range(8)], axis=0
            )
            at = first + j - 8 * shift - 1 + lane_piece
            kept = jnp.where((at >= 0) & (at <= 7), rows, 0.0)
            out_ref[pl.ds(first + j, 1), 0:BAND_ROWS, :] = kept.astype(jnp.bfloat16)[None]


def band_biases(place, pair_act, w_bias, atom_act, atom_token, far_atoms, far_tokens):
    vmem = pl.BlockSpec(memory_space=pltpu.VMEM)
    return pl.pallas_call(
        band_kernel,
        in_specs=[
            pl.BlockSpec(memory_space=pltpu.SMEM),
            pl.BlockSpec(memory_space=pl.ANY),
        ]
        + [vmem] * 5,
        out_specs=[vmem] * 2,
        out_shape=[
            jax.ShapeDtypeStruct((16, BLOCK_ROWS, 128), jnp.bfloat16),
            jax.ShapeDtypeStruct((16, 128), jnp.bfloat16),
        ],
        scratch_shapes=[
            pltpu.VMEM((GROUPS, 16, WINDOW + 2 * EDGE, 128), jnp.bfloat16),
            pltpu.SemaphoreType.DMA((GROUPS,)),
        ],
        cost_estimate=pl.CostEstimate(flops=10**9, bytes_accessed=3 * 10**6, transcendentals=0),
        compiler_params=pltpu.CompilerParams(vmem_limit_bytes=56 * MIB),
        name="band",
    )(
        place, pair_act, w_bias.T, atom_act, atom_token[None, :], far_atoms, far_tokens[None, :]
    )


def atom_kernel(
    place_ref, own_ref, tok_ref, near_ref, gain_ref, wattn_ref, wout_ref,
    wagg_ref, wsingle_ref, atom_out_ref, next_out_ref, shared_ref, token_ref, singles_ref,
    wide, q_scr, k_scr, v_scr, gate_scr,
):
    flat = place_ref[2]
    atoms = own_ref.shape[0]
    heads = 4
    n_query = atoms + QB
    total = place_ref[3]
    col = place_ref[1]
    last = near_ref.shape[0] - 1
    low = BAND_ROWS
    below = jnp.where(col == 0, last, col - 1)
    above = jnp.where(col == last, 0, col + 1)
    from_below = near_ref[below, low : low + 16 + BELOW, :].astype(jnp.float32)
    from_above = near_ref[above, low:, :].astype(jnp.float32)
    wide[0:BELOW, :] = from_below[16:]
    wide[BELOW : BELOW + atoms, :] = own_ref[...].astype(jnp.float32)
    wide[BELOW + atoms :, :] = from_above[16:]
    normed = (normalize(wide[...]) * gain_ref[...]).astype(jnp.bfloat16)
    projected = dot(normed, wattn_ref[...])
    q_scr[...] = projected[BELOW : BELOW + n_query, 0:128].astype(jnp.bfloat16)
    k_scr[...] = projected[:, 128:256].astype(jnp.bfloat16)
    v_scr[...] = projected[:, 256:384].astype(jnp.bfloat16)
    gate_scr[...] = jax.nn.sigmoid(projected[BELOW : BELOW + n_query, 384:512])

    tok_own = tok_ref[0:1, :].astype(jnp.float32)
    tok_below = from_below[0:1] - TOK_DEV
    tok_above = from_above[0:1] + TOK_DEV
    lane = lax.broadcasted_iota(jnp.int32, (8, 128), 1)
    rolled_own = pltpu.roll(jnp.broadcast_to(tok_own, (8, 128)), BELOW, 1)
    rolled_below = pltpu.roll(jnp.broadcast_to(tok_below, (8, 128)), BELOW, 1)
    rolled_above = pltpu.roll(jnp.broadcast_to(tok_above, (8, 128)), BELOW, 1)
    key_tok = jnp.concatenate(
        [
            jnp.where(lane < BELOW, rolled_below, rolled_own)[0:1],
            jnp.where(lane < BELOW, rolled_own, rolled_above)[0:1],
        ],
        axis=1,
    )
    col_own = jnp.transpose(jnp.broadcast_to(tok_own, (128, 128)))
    col_above = jnp.transpose(jnp.broadcast_to(tok_above, (128, 128)))

    band = jnp.sum(near_ref[:, 0:BAND_ROWS, :].astype(jnp.float32), axis=0)
    half = lax.broadcasted_iota(jnp.int32, (BAND_ROWS, 128), 1) < WINDOW
    band = jnp.concatenate([jnp.where(half, band, 0.0), jnp.where(half, 0.0, band)], axis=0)
    slot = (lax.broadcasted_iota(jnp.int32, (128, 256), 0) % WINDOW - 16).astype(jnp.float32)
    pick_key = (slot == key_tok).astype(jnp.bfloat16)
    spread = dot(band.astype(jnp.bfloat16), pick_key).astype(jnp.bfloat16)

    row_head = lax.broadcasted_iota(jnp.int32, (128, 128), 0) // QB
    lane_head = lax.broadcasted_iota(jnp.int32, (128, 128), 1) // 32
    own_head = row_head == lane_head
    entry = lax.broadcasted_iota(jnp.int32, (128, WINDOW), 1)
    entry_tok = (2 * ((entry % 32) // 4) + entry // 32).astype(jnp.float32)
    entry_head = entry % 4 == lax.broadcasted_iota(jnp.int32, (128, WINDOW), 0) // QB
    key_lane = lax.broadcasted_iota(jnp.int32, (128, KW), 1)
    for b in range(n_query // QB):
        at = b * QB
        queries = q_scr[at : at + QB, :]
        stacked = jnp.where(own_head, jnp.concatenate([queries] * heads, axis=0), 0)
        keys = k_scr[at : at + KW, :]
        tok_col = col_own[at : at + QB, 0:WINDOW] if at < atoms else col_above[0:QB, 0:WINDOW]
        pick = (jnp.concatenate([tok_col] * heads, axis=0) == entry_tok) & entry_head
        bias = dot(pick.astype(jnp.bfloat16), spread[:, at : at + KW])
        scores = dot_nt(stacked, keys) * (1.0 / math.sqrt(32)) + bias
        key_index = flat * atoms - BELOW + at + key_lane
        scores = jnp.where((key_index >= 0) & (key_index < total), scores, -jnp.inf)
        exponent = jnp.exp(scores - jnp.max(scores, axis=-1, keepdims=True))
        weights = (exponent / jnp.sum(exponent, axis=-1, keepdims=True)).astype(jnp.bfloat16)
        mixed = jnp.where(own_head, dot(weights, v_scr[at : at + KW, :]), 0.0)
        mixed = (mixed[0:32] + mixed[32:64]) + (mixed[64:96] + mixed[96:128])
        gate_scr[at : at + QB, :] = gate_scr[at : at + QB, :] * mixed
    attended = gate_scr[...].astype(jnp.bfloat16)
    atom_out = (wide[BELOW : BELOW + n_query, :] + dot(attended, wout_ref[...])).astype(
        jnp.bfloat16
    )
    atom_out_ref[...] = atom_out[0:atoms]
    next_out_ref[0:16, :] = atom_out[atoms : atoms + 16]
    next_out_ref[16:, :] = jnp.zeros((atoms - 16, 128), jnp.bfloat16)
    shared_ref[...] = col_own.astype(jnp.bfloat16)
    features = jnp.maximum(dot(atom_out, wagg_ref[...]), 0.0)
    tokens = lax.broadcasted_iota(jnp.int32, (TOK_DEV, 128), 0).astype(jnp.float32)
    member = (tok_own == tokens).astype(jnp.float32)
    member_next = ((tok_above == tokens) & (key_lane[0:TOK_DEV] < QB)).astype(jnp.float32)[:, 0:QB]
    counts = jnp.sum(member, axis=1, keepdims=True) + jnp.sum(member_next, axis=1, keepdims=True)
    totals = dot(member, features[0:atoms], precision=lax.Precision.HIGHEST) + dot(
        member_next, features[atoms:], precision=lax.Precision.HIGHEST
    )
    token_single = (totals / counts).astype(jnp.bfloat16)
    token_ref[...] = token_single
    singles = dot(token_single, wsingle_ref[...]).astype(jnp.bfloat16)
    singles_ref[...] = singles


def atom_part(place, own, tok_rows, near, atom_gain, w_attn, w_out, w_agg, w_single):
    atoms = own.shape[0]
    vmem = pl.BlockSpec(memory_space=pltpu.VMEM)
    return pl.pallas_call(
        atom_kernel,
        in_specs=[pl.BlockSpec(memory_space=pltpu.SMEM)] + [vmem] * 8,
        out_specs=[vmem] * 5,
        out_shape=[
            jax.ShapeDtypeStruct((atoms, 128), jnp.bfloat16),
            jax.ShapeDtypeStruct((atoms, 128), jnp.bfloat16),
            jax.ShapeDtypeStruct((atoms, 128), jnp.bfloat16),
            jax.ShapeDtypeStruct((TOK_DEV, 384), jnp.bfloat16),
            jax.ShapeDtypeStruct((TOK_DEV, 256), jnp.bfloat16),
        ],
        scratch_shapes=[
            pltpu.VMEM((atoms + KW, 128), jnp.float32),
            pltpu.VMEM((atoms + QB, 128), jnp.bfloat16),
            pltpu.VMEM((atoms + KW, 128), jnp.bfloat16),
            pltpu.VMEM((atoms + KW, 128), jnp.bfloat16),
            pltpu.VMEM((atoms + QB, 128), jnp.float32),
        ],
        cost_estimate=pl.CostEstimate(flops=10**9, bytes_accessed=10**6, transcendentals=10**5),
        compiler_params=pltpu.CompilerParams(vmem_limit_bytes=16 * MIB),
        name="atoms",
    )(place, own, tok_rows, near, atom_gain, w_attn, w_out, w_agg, w_single)


def whole(array):
    return pl.BlockSpec(array.shape, lambda i: (0,) * array.ndim)


def halved_gate(w_in_ref, w_in_scr):
    width = w_in_ref.shape[1] // 2
    w_in_scr[:, :width] = w_in_ref[:, :width] * 0.5
    w_in_scr[:, width:] = w_in_ref[:, width:]


def transition(cells, w_in_scr, w_out_ref):
    width = w_out_ref.shape[0]
    wide = cells.reshape(-1, 128).astype(jnp.float32)
    hidden = dot(normalize(wide).astype(jnp.bfloat16), w_in_scr[...])
    gate = hidden[:, :width].astype(jnp.bfloat16)
    up = hidden[:, width:].astype(jnp.bfloat16)
    return wide + dot((gate + gate * jnp.tanh(gate)) * up, w_out_ref[...])


def early_kernel(pair_ref, w_in_ref, w_out_ref, band_ref, out_ref, w_in_scr):
    rows, cols, _ = pair_ref.shape

    @pl.when(pl.program_id(0) == 0)
    def _():
        halved_gate(w_in_ref, w_in_scr)

    step = SUB // cols
    for k in range(0, rows, step):
        moved = transition(pair_ref[k : k + step], w_in_scr, w_out_ref)
        out_ref[k : k + step] = moved.astype(jnp.bfloat16).reshape(step, cols, 128)


def early_part(pair_act, w_in, w_out, band):
    rows, cols, width = pair_act.shape
    block = pl.BlockSpec((EARLY, cols, width), lambda i: (ROWS // EARLY * i, 0, 0))
    cells = rows // ROWS * EARLY * cols
    return pl.pallas_call(
        early_kernel,
        grid=(rows // ROWS,),
        in_specs=[block, whole(w_in), whole(w_out), pl.BlockSpec(memory_space=pl.ANY)],
        out_specs=block,
        out_shape=jax.ShapeDtypeStruct(pair_act.shape, jnp.bfloat16),
        scratch_shapes=[pltpu.VMEM(w_in.shape, jnp.bfloat16)],
        cost_estimate=pl.CostEstimate(
            flops=cells * 196608 * 2, bytes_accessed=cells * 512, transcendentals=0
        ),
        compiler_params=pltpu.CompilerParams(vmem_limit_bytes=WIDE * MIB),
        name="pair_early",
    )(pair_act, w_in, w_out, band)


def last_kernel(
    place_ref, pair_ref, done_ref, w_in_ref, w_out_ref, own_ref, other_ref, col_ref,
    out_ref, w_in_scr, row_scr, col_scr,
):
    i = pl.program_id(0)
    rows, cols, _ = pair_ref.shape

    @pl.when(i == 0)
    def _():
        halved_gate(w_in_ref, w_in_scr)
        col, sender = place_ref[1], place_ref[4]
        half = col // 8
        for block in range(8):
            at = slice(block * TOK_DEV, (block + 1) * TOK_DEV)
            row_at = pl.ds(pl.multiple_of((block ^ (col % 8)) * 16, 16), 16)
            col_at = pl.ds(pl.multiple_of((block ^ sender) * 16, 16), 16)
            own_to = pl.ds(pl.multiple_of(half * 128 + block * 16, 16), 16)
            other_to = pl.ds(pl.multiple_of((1 - half) * 128 + block * 16, 16), 16)
            row_scr[own_to, :] = own_ref[row_at, 0:128].astype(jnp.float32)
            row_scr[other_to, :] = other_ref[row_at, 0:128].astype(jnp.float32)
            col_scr[at, :] = col_ref[col_at, 128:256].astype(jnp.float32)

    base = pl.multiple_of(i * rows, rows)
    col_add = col_scr[...]
    step = SUB // cols
    for k in range(EARLY, rows, step):
        moved = transition(pair_ref[k : k + step], w_in_scr, w_out_ref)
        for s in range(step):
            extra = row_scr[pl.ds(base + k + s, 1), :] + col_add
            out_ref[k + s] = (moved[s * cols : (s + 1) * cols] + extra).astype(jnp.bfloat16)
    for r in range(EARLY):
        extra = row_scr[pl.ds(base + r, 1), :] + col_add
        out_ref[r] = (done_ref[r].astype(jnp.float32) + extra).astype(jnp.bfloat16)


def last_part(place, pair_act, done, w_in, w_out, own, other, col):
    rows, cols, width = pair_act.shape
    block = pl.BlockSpec((ROWS, cols, width), lambda i: (i, 0, 0))
    done_block = pl.BlockSpec((EARLY, cols, width), lambda i: (ROWS // EARLY * i, 0, 0))
    return pl.pallas_call(
        last_kernel,
        grid=(rows // ROWS,),
        in_specs=[pl.BlockSpec(memory_space=pltpu.SMEM), block, done_block]
        + [whole(x) for x in (w_in, w_out, own, other, col)],
        out_specs=block,
        out_shape=jax.ShapeDtypeStruct(pair_act.shape, jnp.bfloat16),
        scratch_shapes=[
            pltpu.VMEM(w_in.shape, jnp.bfloat16),
            pltpu.VMEM((rows, width), jnp.float32),
            pltpu.VMEM((cols, width), jnp.float32),
        ],
        cost_estimate=pl.CostEstimate(
            flops=rows * cols * 196608 * 2, bytes_accessed=rows * cols * 512, transcendentals=0
        ),
        compiler_params=pltpu.CompilerParams(vmem_limit_bytes=WIDE * MIB),
        name="pair_last",
    )(place, pair_act, done, w_in, w_out, own, other, col)


def chip_of(row, col):
    x_lo, z = divmod(row, 4)
    y, rest = divmod(col, 4)
    return (2 * (rest // 2) + x_lo, y, z)


def hops(one, other):
    return sum(min((a - b) % 4, (b - a) % 4) for a, b in zip(one, other))


def assigned(costs, most):
    owner = {}

    def place(source, seen):
        for target in sorted(range(len(costs)), key=lambda t: costs[source][t]):
            if costs[source][target] <= most and target not in seen:
                seen.add(target)
                if target not in owner or place(owner[target], seen):
                    owner[target] = source
                    return True
        return False

    for source in range(len(costs)):
        if not place(source, set()):
            return None
    return {source: target for target, source in owner.items()}


def column_turn():
    pairs = []
    for row in range(8):
        for half in range(2):
            column = 2 * row + half
            costs = [
                [hops(chip_of(row, 8 * half + k), chip_of(target, column)) for target in range(8)]
                for k in range(8)
            ]
            most = 0
            while assigned(costs, most) is None:
                most += 1
            found = assigned(costs, most)
            pairs += [(16 * row + 8 * half + k, 16 * found[k] + column) for k in range(8)]
    return pairs


def on_device(
    pair_act, atom_act, atom_token, atom_gain, w_attn, w_out, w_bias, w_trans_in, w_trans_out,
    w_agg, w_single,
):
    atom_n = atom_act.shape[0]
    n_row, n_col = lax.axis_size("row"), lax.axis_size("col")
    devices = n_row * n_col
    row_index, col_index = lax.axis_index("row"), lax.axis_index("col")
    flat = row_index * n_col + col_index
    both = ("row", "col")
    up = [(i, i + 1) for i in range(devices - 1)]
    turn = column_turn()
    senders = np.zeros(devices, np.int32)
    for source, target in turn:
        senders[target] = source % 8
    place = jnp.stack(
        [row_index, col_index, flat, jnp.int32(devices * atom_n), jnp.asarray(senders)[flat]]
    ).astype(jnp.int32)
    ends = [(n_col * (i + 1) - 1, n_col * (i + 2) - 1) for i in range(n_row - 1)]
    ends += [(n_col * (i + 1), n_col * i) for i in range(n_row - 1)]

    far_atoms = lax.ppermute(atom_act, both, ends)
    far_tokens = lax.ppermute(atom_token, both, ends)
    band, tok_rows = band_biases(
        place, pair_act, w_bias, atom_act, atom_token, far_atoms, far_tokens
    )
    near = lax.all_to_all(band, "col", 0, 0, tiled=True)
    done = early_part(pair_act, w_trans_in, w_trans_out, band)
    near = lax.optimization_barrier((near, done))[0]
    atom_main, next_out, shared, token_single, singles = atom_part(
        place, atom_act, tok_rows, near, atom_gain[None, :], w_attn, w_out, w_agg, w_single
    )
    held = singles
    for k in range(3):
        pairs = [(i, i ^ (1 << k)) for i in range(n_col)]
        held = jnp.concatenate([held, lax.ppermute(held, "col", pairs)])
    col_all = lax.ppermute(held, both, turn)
    other = lax.ppermute(held, "col", [(i, i ^ 8) for i in range(n_col)])
    from_below = lax.ppermute(next_out, both, up)
    pair_out = last_part(
        place, pair_act, done, w_trans_in, w_trans_out, held, other, col_all
    )
    from_below = lax.optimization_barrier((from_below, pair_out))[0]
    atom_out = jnp.where(shared < 0, from_below, atom_main)
    return (atom_out, token_single, pair_out)


def solution(mesh):
    both = P(("row", "col"), None)
    return jax.shard_map(
        on_device,
        mesh=mesh,
        in_specs=(P("row", "col", None), both, P(("row", "col"))) + (P(),) * 8,
        out_specs=(both, both, P("row", "col", None)),
        check_vma=False,
    )
```

```python
import functools
import math

import jax
import jax.numpy as jnp
import numpy as np
from jax import lax
from jax.experimental import pallas as pl
from jax.experimental.pallas import tpu as pltpu
from jax.sharding import PartitionSpec as P

SPAN = 10
QB = 32
KW = 128
TOK_DEV = 16
BELOW = (KW - QB) // 2
ABOVE = KW - BELOW
WINDOW = 64
GROUPS = 9
BAND_ROWS = 32
EDGE = 48
BLOCK_ROWS = BAND_ROWS + 16 + ABOVE
BATCH = 3
MIB = 1024 * 1024
WIDE = 50
ROWS = 64
EARLY = 16
SUB = 512


def normalize(values):
    centre = values - jnp.mean(values, axis=-1, keepdims=True)
    spread = jnp.mean(centre * centre, axis=-1, keepdims=True)
    return centre * lax.rsqrt(spread + 1e-05)


def dot(a, b, **kw):
    return jnp.dot(a, b, preferred_element_type=jnp.float32, **kw)


def dot_nt(a, b):
    return lax.dot_general(a, b, (((1,), (1,)), ((), ())), preferred_element_type=jnp.float32)


def band_kernel(
    place_ref, pair_ref, weight_ref, atom_ref, token_ref, far_atom_ref, far_token_ref, out_ref,
    tok_ref, cells, sems,
):
    row, col = place_ref[0], place_ref[1]
    shift = col - 2 * row
    first = jnp.clip(8 * shift - 1, 0, 7)
    copies = []
    for j in range(GROUPS):
        group = first + j
        start = group - 8 * shift - 1
        begin = jnp.clip(start, 0, 4)
        at = jnp.clip(EDGE // 16 + begin - start, 0, 2 * EDGE // 16)
        copy = pltpu.make_async_copy(
            pair_ref.at[
                pl.ds(pl.multiple_of(group * 16, 16), 16),
                pl.ds(pl.multiple_of(begin * 16, 16), WINDOW),
                :,
            ],
            cells.at[j, :, pl.ds(pl.multiple_of(at * 16, 16), WINDOW), :],
            sems.at[j],
        )
        copy.start()
        copies.append(copy)
    out_ref[:, 0:BAND_ROWS, :] = jnp.zeros((out_ref.shape[0], BAND_ROWS, 128), jnp.bfloat16)
    atoms = atom_ref.shape[0]
    token_rel = (token_ref[...] - place_ref[2] * TOK_DEV).astype(jnp.float32)
    tok_rows = jnp.broadcast_to(token_rel, (16, 128)).astype(jnp.bfloat16)
    tok_ref[...] = tok_rows
    low = BAND_ROWS
    last = out_ref.shape[0] - 1

    def to_above(ref, rows, source):
        ref[low : low + 16, :] = rows
        ref[low + 16 : low + 16 + BELOW, :] = source[atoms - BELOW :, :]

    def to_below(ref, rows, source):
        ref[low : low + 16, :] = rows
        ref[low + 16 : low + 16 + ABOVE, :] = source[0:ABOVE, :]

    @pl.when(col < last)
    def _():
        to_above(out_ref.at[col + 1], tok_rows, atom_ref)

    @pl.when(col > 0)
    def _():
        to_below(out_ref.at[col - 1], tok_rows, atom_ref)

    def far_rows(first_token):
        far = (far_token_ref[...] - first_token).astype(jnp.float32)
        return jnp.broadcast_to(far, (16, 128)).astype(jnp.bfloat16)

    wide_row = TOK_DEV * (last + 1)

    @pl.when(col == last)
    def _():
        to_above(out_ref.at[0], far_rows(place_ref[2] * TOK_DEV - wide_row), far_atom_ref)

    @pl.when(col == 0)
    def _():
        to_below(out_ref.at[last], far_rows(place_ref[2] * TOK_DEV + wide_row), far_atom_ref)

    weight = jnp.concatenate(
        [weight_ref[...].astype(jnp.float32), jnp.zeros((12, 128), jnp.float32)], axis=0
    ).astype(jnp.bfloat16)
    lane_piece = (lax.broadcasted_iota(jnp.int32, (BAND_ROWS, 128), 1) % WINDOW) // 16
    for j0 in range(0, GROUPS, BATCH):
        for j in range(j0, j0 + BATCH):
            copies[j].wait()
        flat = cells[j0 : j0 + BATCH, :, EDGE : EDGE + WINDOW, :].reshape(-1, 128)
        normed = normalize(flat.astype(jnp.float32)).astype(jnp.bfloat16)
        biases = dot_nt(weight, normed)
        for j in range(j0, j0 + BATCH):
            off = (j - j0) * 8
            rows = jnp.concatenate(
                [biases[0:4, 128 * (off + i) : 128 * (off + i + 1)] for i in range(8)], axis=0
            )
            at = first + j - 8 * shift - 1 + lane_piece
            kept = jnp.where((at >= 0) & (at <= 7), rows, 0.0)
            out_ref[pl.ds(first + j, 1), 0:BAND_ROWS, :] = kept.astype(jnp.bfloat16)[None]


def band_biases(place, pair_act, w_bias, atom_act, atom_token, far_atoms, far_tokens):
    vmem = pl.BlockSpec(memory_space=pltpu.VMEM)
    return pl.pallas_call(
        band_kernel,
        in_specs=[
            pl.BlockSpec(memory_space=pltpu.SMEM),
            pl.BlockSpec(memory_space=pl.ANY),
        ]
        + [vmem] * 5,
        out_specs=[vmem] * 2,
        out_shape=[
            jax.ShapeDtypeStruct((16, BLOCK_ROWS, 128), jnp.bfloat16),
            jax.ShapeDtypeStruct((16, 128), jnp.bfloat16),
        ],
        scratch_shapes=[
            pltpu.VMEM((GROUPS, 16, WINDOW + 2 * EDGE, 128), jnp.bfloat16),
            pltpu.SemaphoreType.DMA((GROUPS,)),
        ],
        cost_estimate=pl.CostEstimate(flops=10**9, bytes_accessed=3 * 10**6, transcendentals=0),
        compiler_params=pltpu.CompilerParams(vmem_limit_bytes=56 * MIB),
        name="band",
    )(
        place, pair_act, w_bias.T, atom_act, atom_token[None, :], far_atoms, far_tokens[None, :]
    )


def atom_kernel(
    place_ref, own_ref, tok_ref, near_ref, gain_ref, wattn_ref, wout_ref,
    wagg_ref, wsingle_ref, atom_out_ref, next_out_ref, shared_ref, token_ref, singles_ref,
    wide, q_scr, k_scr, v_scr, gate_scr,
):
    flat = place_ref[2]
    atoms = own_ref.shape[0]
    heads = 4
    n_query = atoms + QB
    total = place_ref[3]
    col = place_ref[1]
    last = near_ref.shape[0] - 1
    low = BAND_ROWS
    below = jnp.where(col == 0, last, col - 1)
    above = jnp.where(col == last, 0, col + 1)
    from_below = near_ref[below, low : low + 16 + BELOW, :].astype(jnp.float32)
    from_above = near_ref[above, low:, :].astype(jnp.float32)
    wide[0:BELOW, :] = from_below[16:]
    wide[BELOW : BELOW + atoms, :] = own_ref[...].astype(jnp.float32)
    wide[BELOW + atoms :, :] = from_above[16:]
    normed = (normalize(wide[...]) * gain_ref[...]).astype(jnp.bfloat16)
    projected = dot(normed, wattn_ref[...])
    q_scr[...] = projected[BELOW : BELOW + n_query, 0:128].astype(jnp.bfloat16)
    k_scr[...] = projected[:, 128:256].astype(jnp.bfloat16)
    v_scr[...] = projected[:, 256:384].astype(jnp.bfloat16)
    gate_scr[...] = jax.nn.sigmoid(projected[BELOW : BELOW + n_query, 384:512])

    tok_own = tok_ref[0:1, :].astype(jnp.float32)
    tok_below = from_below[0:1] - TOK_DEV
    tok_above = from_above[0:1] + TOK_DEV
    lane = lax.broadcasted_iota(jnp.int32, (8, 128), 1)
    rolled_own = pltpu.roll(jnp.broadcast_to(tok_own, (8, 128)), BELOW, 1)
    rolled_below = pltpu.roll(jnp.broadcast_to(tok_below, (8, 128)), BELOW, 1)
    rolled_above = pltpu.roll(jnp.broadcast_to(tok_above, (8, 128)), BELOW, 1)
    key_tok = jnp.concatenate(
        [
            jnp.where(lane < BELOW, rolled_below, rolled_own)[0:1],
            jnp.where(lane < BELOW, rolled_own, rolled_above)[0:1],
        ],
        axis=1,
    )
    col_own = jnp.transpose(jnp.broadcast_to(tok_own, (128, 128)))
    col_above = jnp.transpose(jnp.broadcast_to(tok_above, (128, 128)))

    band = jnp.sum(near_ref[:, 0:BAND_ROWS, :].astype(jnp.float32), axis=0)
    half = lax.broadcasted_iota(jnp.int32, (BAND_ROWS, 128), 1) < WINDOW
    band = jnp.concatenate([jnp.where(half, band, 0.0), jnp.where(half, 0.0, band)], axis=0)
    slot = (lax.broadcasted_iota(jnp.int32, (128, 256), 0) % WINDOW - 16).astype(jnp.float32)
    pick_key = (slot == key_tok).astype(jnp.bfloat16)
    spread = dot(band.astype(jnp.bfloat16), pick_key).astype(jnp.bfloat16)

    row_head = lax.broadcasted_iota(jnp.int32, (128, 128), 0) // QB
    lane_head = lax.broadcasted_iota(jnp.int32, (128, 128), 1) // 32
    own_head = row_head == lane_head
    entry = lax.broadcasted_iota(jnp.int32, (128, WINDOW), 1)
    entry_tok = (2 * ((entry % 32) // 4) + entry // 32).astype(jnp.float32)
    entry_head = entry % 4 == lax.broadcasted_iota(jnp.int32, (128, WINDOW), 0) // QB
    key_lane = lax.broadcasted_iota(jnp.int32, (128, KW), 1)
    for b in range(n_query // QB):
        at = b * QB
        queries = q_scr[at : at + QB, :]
        stacked = jnp.where(own_head, jnp.concatenate([queries] * heads, axis=0), 0)
        keys = k_scr[at : at + KW, :]
        tok_col = col_own[at : at + QB, 0:WINDOW] if at < atoms else col_above[0:QB, 0:WINDOW]
        pick = (jnp.concatenate([tok_col] * heads, axis=0) == entry_tok) & entry_head
        bias = dot(pick.astype(jnp.bfloat16), spread[:, at : at + KW])
        scores = dot_nt(stacked, keys) * (1.0 / math.sqrt(32)) + bias
        key_index = flat * atoms - BELOW + at + key_lane
        scores = jnp.where((key_index >= 0) & (key_index < total), scores, -jnp.inf)
        exponent = jnp.exp(scores - jnp.max(scores, axis=-1, keepdims=True))
        weights = (exponent / jnp.sum(exponent, axis=-1, keepdims=True)).astype(jnp.bfloat16)
        mixed = jnp.where(own_head, dot(weights, v_scr[at : at + KW, :]), 0.0)
        mixed = (mixed[0:32] + mixed[32:64]) + (mixed[64:96] + mixed[96:128])
        gate_scr[at : at + QB, :] = gate_scr[at : at + QB, :] * mixed
    attended = gate_scr[...].astype(jnp.bfloat16)
    atom_out = (wide[BELOW : BELOW + n_query, :] + dot(attended, wout_ref[...])).astype(
        jnp.bfloat16
    )
    atom_out_ref[...] = atom_out[0:atoms]
    next_out_ref[0:16, :] = atom_out[atoms : atoms + 16]
    next_out_ref[16:, :] = jnp.zeros((atoms - 16, 128), jnp.bfloat16)
    shared_ref[...] = col_own.astype(jnp.bfloat16)
    features = jnp.maximum(dot(atom_out, wagg_ref[...]), 0.0)
    tokens = lax.broadcasted_iota(jnp.int32, (TOK_DEV, 128), 0).astype(jnp.float32)
    member = (tok_own == tokens).astype(jnp.float32)
    member_next = ((tok_above == tokens) & (key_lane[0:TOK_DEV] < QB)).astype(jnp.float32)[:, 0:QB]
    counts = jnp.sum(member, axis=1, keepdims=True) + jnp.sum(member_next, axis=1, keepdims=True)
    totals = dot(member, features[0:atoms], precision=lax.Precision.HIGHEST) + dot(
        member_next, features[atoms:], precision=lax.Precision.HIGHEST
    )
    token_single = (totals / counts).astype(jnp.bfloat16)
    token_ref[...] = token_single
    singles = dot(token_single, wsingle_ref[...]).astype(jnp.bfloat16)
    singles_ref[...] = singles


def atom_part(place, own, tok_rows, near, atom_gain, w_attn, w_out, w_agg, w_single):
    atoms = own.shape[0]
    vmem = pl.BlockSpec(memory_space=pltpu.VMEM)
    return pl.pallas_call(
        atom_kernel,
        in_specs=[pl.BlockSpec(memory_space=pltpu.SMEM)] + [vmem] * 8,
        out_specs=[vmem] * 5,
        out_shape=[
            jax.ShapeDtypeStruct((atoms, 128), jnp.bfloat16),
            jax.ShapeDtypeStruct((atoms, 128), jnp.bfloat16),
            jax.ShapeDtypeStruct((atoms, 128), jnp.bfloat16),
            jax.ShapeDtypeStruct((TOK_DEV, 384), jnp.bfloat16),
            jax.ShapeDtypeStruct((TOK_DEV, 256), jnp.bfloat16),
        ],
        scratch_shapes=[
            pltpu.VMEM((atoms + KW, 128), jnp.float32),
            pltpu.VMEM((atoms + QB, 128), jnp.bfloat16),
            pltpu.VMEM((atoms + KW, 128), jnp.bfloat16),
            pltpu.VMEM((atoms + KW, 128), jnp.bfloat16),
            pltpu.VMEM((atoms + QB, 128), jnp.float32),
        ],
        cost_estimate=pl.CostEstimate(flops=10**9, bytes_accessed=10**6, transcendentals=10**5),
        compiler_params=pltpu.CompilerParams(vmem_limit_bytes=16 * MIB),
        name="atoms",
    )(place, own, tok_rows, near, atom_gain, w_attn, w_out, w_agg, w_single)


def whole(array):
    return pl.BlockSpec(array.shape, lambda i: (0,) * array.ndim)


def halved_gate(w_in_ref, w_in_scr):
    width = w_in_ref.shape[1] // 2
    w_in_scr[:, :width] = w_in_ref[:, :width] * 0.5
    w_in_scr[:, width:] = w_in_ref[:, width:]


def transition(cells, w_in_scr, w_out_ref):
    width = w_out_ref.shape[0]
    wide = cells.reshape(-1, 128).astype(jnp.float32)
    hidden = dot(normalize(wide).astype(jnp.bfloat16), w_in_scr[...])
    gate = hidden[:, :width].astype(jnp.bfloat16)
    up = hidden[:, width:].astype(jnp.bfloat16)
    return wide + dot((gate + gate * jnp.tanh(gate)) * up, w_out_ref[...])


def early_kernel(pair_ref, w_in_ref, w_out_ref, band_ref, out_ref, w_in_scr):
    rows, cols, _ = pair_ref.shape

    @pl.when(pl.program_id(0) == 0)
    def _():
        halved_gate(w_in_ref, w_in_scr)

    step = SUB // cols
    for k in range(0, rows, step):
        moved = transition(pair_ref[k : k + step], w_in_scr, w_out_ref)
        out_ref[k : k + step] = moved.astype(jnp.bfloat16).reshape(step, cols, 128)


def early_part(pair_act, w_in, w_out, band):
    rows, cols, width = pair_act.shape
    block = pl.BlockSpec((EARLY, cols, width), lambda i: (ROWS // EARLY * i, 0, 0))
    cells = rows // ROWS * EARLY * cols
    return pl.pallas_call(
        early_kernel,
        grid=(rows // ROWS,),
        in_specs=[block, whole(w_in), whole(w_out), pl.BlockSpec(memory_space=pl.ANY)],
        out_specs=block,
        out_shape=jax.ShapeDtypeStruct(pair_act.shape, jnp.bfloat16),
        scratch_shapes=[pltpu.VMEM(w_in.shape, jnp.bfloat16)],
        cost_estimate=pl.CostEstimate(
            flops=cells * 196608 * 2, bytes_accessed=cells * 512, transcendentals=0
        ),
        compiler_params=pltpu.CompilerParams(vmem_limit_bytes=WIDE * MIB),
        name="pair_early",
    )(pair_act, w_in, w_out, band)


def last_kernel(
    place_ref, sender_ref, pair_ref, done_ref, w_in_ref, w_out_ref, own_ref, other_ref, col_ref,
    out_ref, w_in_scr, row_scr, col_scr,
):
    i = pl.program_id(0)
    rows, cols, _ = pair_ref.shape

    @pl.when(i == 0)
    def _():
        halved_gate(w_in_ref, w_in_scr)
        col, sender = place_ref[1], sender_ref[place_ref[2]]
        half = col // 8
        for block in range(8):
            at = slice(block * TOK_DEV, (block + 1) * TOK_DEV)
            row_at = pl.ds(pl.multiple_of((block ^ (col % 8)) * 16, 16), 16)
            col_at = pl.ds(pl.multiple_of((block ^ sender) * 16, 16), 16)
            own_to = pl.ds(pl.multiple_of(half * 128 + block * 16, 16), 16)
            other_to = pl.ds(pl.multiple_of((1 - half) * 128 + block * 16, 16), 16)
            row_scr[own_to, :] = own_ref[row_at, 0:128].astype(jnp.float32)
            row_scr[other_to, :] = other_ref[row_at, 0:128].astype(jnp.float32)
            col_scr[at, :] = col_ref[col_at, 128:256].astype(jnp.float32)

    base = pl.multiple_of(i * rows, rows)
    col_add = col_scr[...]
    step = SUB // cols
    for k in range(EARLY, rows, step):
        moved = transition(pair_ref[k : k + step], w_in_scr, w_out_ref)
        for s in range(step):
            extra = row_scr[pl.ds(base + k + s, 1), :] + col_add
            out_ref[k + s] = (moved[s * cols : (s + 1) * cols] + extra).astype(jnp.bfloat16)
    for r in range(EARLY):
        extra = row_scr[pl.ds(base + r, 1), :] + col_add
        out_ref[r] = (done_ref[r].astype(jnp.float32) + extra).astype(jnp.bfloat16)


def last_part(place, senders, pair_act, done, w_in, w_out, own, other, col):
    rows, cols, width = pair_act.shape
    block = pl.BlockSpec((ROWS, cols, width), lambda i: (i, 0, 0))
    done_block = pl.BlockSpec((EARLY, cols, width), lambda i: (ROWS // EARLY * i, 0, 0))
    return pl.pallas_call(
        last_kernel,
        grid=(rows // ROWS,),
        in_specs=[pl.BlockSpec(memory_space=pltpu.SMEM)] * 2
        + [block, done_block]
        + [whole(x) for x in (w_in, w_out, own, other, col)],
        out_specs=block,
        out_shape=jax.ShapeDtypeStruct(pair_act.shape, jnp.bfloat16),
        scratch_shapes=[
            pltpu.VMEM(w_in.shape, jnp.bfloat16),
            pltpu.VMEM((rows, width), jnp.float32),
            pltpu.VMEM((cols, width), jnp.float32),
        ],
        cost_estimate=pl.CostEstimate(
            flops=rows * cols * 196608 * 2, bytes_accessed=rows * cols * 512, transcendentals=0
        ),
        compiler_params=pltpu.CompilerParams(vmem_limit_bytes=WIDE * MIB),
        name="pair_last",
    )(place, senders, pair_act, done, w_in, w_out, own, other, col)


def chip_of(row, col):
    x_lo, z = divmod(row, 4)
    y, rest = divmod(col, 4)
    return (2 * (rest // 2) + x_lo, y, z)


def hops(one, other):
    return sum(min((a - b) % 4, (b - a) % 4) for a, b in zip(one, other))


def assigned(costs, most):
    owner = {}

    def place(source, seen):
        for target in sorted(range(len(costs)), key=lambda t: costs[source][t]):
            if costs[source][target] <= most and target not in seen:
                seen.add(target)
                if target not in owner or place(owner[target], seen):
                    owner[target] = source
                    return True
        return False

    for source in range(len(costs)):
        if not place(source, set()):
            return None
    return {source: target for target, source in owner.items()}


def column_turn():
    pairs = []
    for row in range(8):
        for half in range(2):
            column = 2 * row + half
            costs = [
                [hops(chip_of(row, 8 * half + k), chip_of(target, column)) for target in range(8)]
                for k in range(8)
            ]
            most = 0
            while assigned(costs, most) is None:
                most += 1
            found = assigned(costs, most)
            pairs += [(16 * row + 8 * half + k, 16 * found[k] + column) for k in range(8)]
    return pairs


def on_device(
    pair_act, atom_act, atom_token, atom_gain, w_attn, w_out, w_bias, w_trans_in, w_trans_out,
    w_agg, w_single,
):
    atom_n = atom_act.shape[0]
    n_row, n_col = lax.axis_size("row"), lax.axis_size("col")
    devices = n_row * n_col
    row_index, col_index = lax.axis_index("row"), lax.axis_index("col")
    flat = row_index * n_col + col_index
    both = ("row", "col")
    up = [(i, i + 1) for i in range(devices - 1)]
    turn = column_turn()
    senders = np.zeros(devices, np.int32)
    for source, target in turn:
        senders[target] = source % 8
    place = jnp.stack([row_index, col_index, flat, jnp.int32(devices * atom_n)]).astype(jnp.int32)
    ends = [(n_col * (i + 1) - 1, n_col * (i + 2) - 1) for i in range(n_row - 1)]
    ends += [(n_col * (i + 1), n_col * i) for i in range(n_row - 1)]

    far_atoms = lax.ppermute(atom_act, both, ends)
    far_tokens = lax.ppermute(atom_token, both, ends)
    band, tok_rows = band_biases(
        place, pair_act, w_bias, atom_act, atom_token, far_atoms, far_tokens
    )
    near = lax.all_to_all(band, "col", 0, 0, tiled=True)
    done = early_part(pair_act, w_trans_in, w_trans_out, band)
    near = lax.optimization_barrier((near, done))[0]
    atom_main, next_out, shared, token_single, singles = atom_part(
        place, atom_act, tok_rows, near, atom_gain[None, :], w_attn, w_out, w_agg, w_single
    )
    def swapped(value, bits):
        return lax.ppermute(value, "col", [(i, i ^ bits) for i in range(n_col)])

    held = jnp.concatenate([singles, swapped(singles, 1)])
    held = jnp.concatenate([held] + [swapped(held, bits) for bits in (2, 4, 6)])
    col_all = lax.ppermute(held, both, turn)
    other = lax.ppermute(held, "col", [(i, i ^ 8) for i in range(n_col)])
    from_below = lax.ppermute(next_out, both, up)
    pair_out = last_part(
        place, jnp.asarray(senders), pair_act, done, w_trans_in, w_trans_out, held, other, col_all
    )
    from_below = lax.optimization_barrier((from_below, pair_out))[0]
    atom_out = jnp.where(shared < 0, from_below, atom_main)
    return (atom_out, token_single, pair_out)


def solution(mesh):
    both = P(("row", "col"), None)
    return jax.shard_map(
        on_device,
        mesh=mesh,
        in_specs=(P("row", "col", None), both, P(("row", "col"))) + (P(),) * 8,
        out_specs=(both, both, P("row", "col", None)),
        check_vma=False,
    )
```

```python
import functools
import math

import jax
import jax.numpy as jnp
import numpy as np
from jax import lax
from jax.experimental import pallas as pl
from jax.experimental.pallas import tpu as pltpu
from jax.sharding import PartitionSpec as P

SPAN = 10
QB = 32
KW = 128
TOK_DEV = 16
BELOW = (KW - QB) // 2
ABOVE = KW - BELOW
WINDOW = 64
GROUPS = 9
BAND_ROWS = 32
EDGE = 48
BLOCK_ROWS = BAND_ROWS + 16 + ABOVE
BATCH = 3
MIB = 1024 * 1024
WIDE = 50
ROWS = 64
EARLY = 16
SUB = 512


def normalize(values):
    centre = values - jnp.mean(values, axis=-1, keepdims=True)
    spread = jnp.mean(centre * centre, axis=-1, keepdims=True)
    return centre * lax.rsqrt(spread + 1e-05)


def dot(a, b, **kw):
    return jnp.dot(a, b, preferred_element_type=jnp.float32, **kw)


def dot_nt(a, b):
    return lax.dot_general(a, b, (((1,), (1,)), ((), ())), preferred_element_type=jnp.float32)


def band_kernel(
    pair_ref, weight_hbm, atom_hbm, token_hbm, out_ref, cross_ref, tok_ref, cells, weight_ref,
    atom_ref, token_ref, sems, small_sems,
):
    row, col = lax.axis_index("row"), lax.axis_index("col")
    flat_index = row * lax.axis_size("col") + col
    shift = col - 2 * row
    first = jnp.clip(8 * shift - 1, 0, 7)
    small = [
        pltpu.make_async_copy(source, target, small_sems.at[i])
        for i, (source, target) in enumerate(
            [(atom_hbm, atom_ref), (token_hbm, token_ref), (weight_hbm, weight_ref)]
        )
    ]
    for copy in small:
        copy.start()
    copies = []
    for j in range(GROUPS):
        group = first + j
        start = group - 8 * shift - 1
        begin = jnp.clip(start, 0, 4)
        at = jnp.clip(EDGE // 16 + begin - start, 0, 2 * EDGE // 16)
        copy = pltpu.make_async_copy(
            pair_ref.at[
                pl.ds(pl.multiple_of(group * 16, 16), 16),
                pl.ds(pl.multiple_of(begin * 16, 16), WINDOW),
                :,
            ],
            cells.at[j, :, pl.ds(pl.multiple_of(at * 16, 16), WINDOW), :],
            sems.at[j],
        )
        copy.start()
        copies.append(copy)
    out_ref[:, 0:BAND_ROWS, :] = jnp.zeros((out_ref.shape[0], BAND_ROWS, 128), jnp.bfloat16)
    for copy in small:
        copy.wait()
    atoms = atom_ref.shape[0]
    token_rel = (token_ref[...] - flat_index * TOK_DEV).astype(jnp.float32)
    tok_rows = jnp.broadcast_to(token_rel, (16, 128)).astype(jnp.bfloat16)
    tok_ref[...] = tok_rows
    low = BAND_ROWS
    last = out_ref.shape[0] - 1

    def to_above(ref, at):
        ref[at : at + 16, :] = tok_rows
        ref[at + 16 : at + 16 + BELOW, :] = atom_ref[atoms - BELOW :, :]

    def to_below(ref, at):
        ref[at : at + 16, :] = tok_rows
        ref[at + 16 : at + 16 + ABOVE, :] = atom_ref[0:ABOVE, :]

    to_above(out_ref.at[jnp.minimum(col + 1, last)], low)
    to_below(out_ref.at[jnp.maximum(col - 1, 0)], low)

    @pl.when(col == last)
    def _():
        to_above(cross_ref, 0)
        to_below(out_ref.at[last - 1], low)

    @pl.when(col == 0)
    def _():
        to_below(cross_ref, 0)
        to_above(out_ref.at[1], low)

    weight = jnp.concatenate(
        [weight_ref[...].astype(jnp.float32), jnp.zeros((12, 128), jnp.float32)], axis=0
    ).astype(jnp.bfloat16)
    lane_piece = (lax.broadcasted_iota(jnp.int32, (BAND_ROWS, 128), 1) % WINDOW) // 16
    for j0 in range(0, GROUPS, BATCH):
        for j in range(j0, j0 + BATCH):
            copies[j].wait()
        flat = cells[j0 : j0 + BATCH, :, EDGE : EDGE + WINDOW, :].reshape(-1, 128)
        normed = normalize(flat.astype(jnp.float32)).astype(jnp.bfloat16)
        biases = dot_nt(weight, normed)
        for j in range(j0, j0 + BATCH):
            off = (j - j0) * 8
            rows = jnp.concatenate(
                [biases[0:4, 128 * (off + i) : 128 * (off + i + 1)] for i in range(8)], axis=0
            )
            at = first + j - 8 * shift - 1 + lane_piece
            kept = jnp.where((at >= 0) & (at <= 7), rows, 0.0)
            out_ref[pl.ds(first + j, 1), 0:BAND_ROWS, :] = kept.astype(jnp.bfloat16)[None]


def band_biases(pair_act, w_bias, atom_act, atom_token):
    vmem = pl.BlockSpec(memory_space=pltpu.VMEM)
    return pl.pallas_call(
        band_kernel,
        in_specs=[pl.BlockSpec(memory_space=pltpu.HBM)] * 4,
        out_specs=[vmem] * 3,
        out_shape=[
            jax.ShapeDtypeStruct((16, BLOCK_ROWS, 128), jnp.bfloat16),
            jax.ShapeDtypeStruct((16 + ABOVE, 128), jnp.bfloat16),
            jax.ShapeDtypeStruct((16, 128), jnp.bfloat16),
        ],
        scratch_shapes=[
            pltpu.VMEM((GROUPS, 16, WINDOW + 2 * EDGE, 128), jnp.bfloat16),
            pltpu.VMEM((4, 128), jnp.bfloat16),
            pltpu.VMEM(atom_act.shape, jnp.bfloat16),
            pltpu.VMEM((1, atom_act.shape[0]), jnp.int32),
            pltpu.SemaphoreType.DMA((GROUPS,)),
            pltpu.SemaphoreType.DMA((3,)),
        ],
        cost_estimate=pl.CostEstimate(flops=10**9, bytes_accessed=3 * 10**6, transcendentals=0),
        compiler_params=pltpu.CompilerParams(vmem_limit_bytes=WIDE * MIB),
        name="band",
    )(pair_act, w_bias.T, atom_act, atom_token[None, :])


def atom_kernel(
    cross_ref, own_ref, tok_ref, near_ref, gain_ref, wattn_ref, wout_ref,
    wagg_ref, wsingle_ref, atom_out_ref, next_out_ref, shared_ref, token_ref, singles_ref,
    wide, q_scr, k_scr, v_scr, gate_scr,
):
    n_col = lax.axis_size("col")
    col = lax.axis_index("col")
    flat = lax.axis_index("row") * n_col + col
    atoms = own_ref.shape[0]
    heads = 4
    n_query = atoms + QB
    total = lax.axis_size("row") * n_col * atoms
    last = near_ref.shape[0] - 1
    low = BAND_ROWS
    from_below = near_ref[jnp.maximum(col - 1, 0), low : low + 16 + BELOW, :].astype(jnp.float32)
    from_above = near_ref[jnp.minimum(col + 1, last), low:, :].astype(jnp.float32)
    cross = cross_ref[...].astype(jnp.float32)
    from_below = jnp.where(col == 0, cross[0 : 16 + BELOW], from_below)
    from_above = jnp.where(col == last, cross, from_above)
    wide[0:BELOW, :] = from_below[16:]
    wide[BELOW : BELOW + atoms, :] = own_ref[...].astype(jnp.float32)
    wide[BELOW + atoms :, :] = from_above[16:]
    normed = (normalize(wide[...]) * gain_ref[...]).astype(jnp.bfloat16)
    projected = dot(normed, wattn_ref[...])
    q_scr[...] = projected[BELOW : BELOW + n_query, 0:128].astype(jnp.bfloat16)
    k_scr[...] = projected[:, 128:256].astype(jnp.bfloat16)
    v_scr[...] = projected[:, 256:384].astype(jnp.bfloat16)
    gate_scr[...] = jax.nn.sigmoid(projected[BELOW : BELOW + n_query, 384:512])

    tok_own = tok_ref[0:1, :].astype(jnp.float32)
    tok_below = from_below[0:1] - TOK_DEV
    tok_above = from_above[0:1] + TOK_DEV
    lane = lax.broadcasted_iota(jnp.int32, (8, 128), 1)
    rolled_own = pltpu.roll(jnp.broadcast_to(tok_own, (8, 128)), BELOW, 1)
    rolled_below = pltpu.roll(jnp.broadcast_to(tok_below, (8, 128)), BELOW, 1)
    rolled_above = pltpu.roll(jnp.broadcast_to(tok_above, (8, 128)), BELOW, 1)
    key_tok = jnp.concatenate(
        [
            jnp.where(lane < BELOW, rolled_below, rolled_own)[0:1],
            jnp.where(lane < BELOW, rolled_own, rolled_above)[0:1],
        ],
        axis=1,
    )
    col_own = jnp.transpose(jnp.broadcast_to(tok_own, (128, 128)))
    col_above = jnp.transpose(jnp.broadcast_to(tok_above, (128, 128)))

    band = jnp.sum(near_ref[:, 0:BAND_ROWS, :].astype(jnp.float32), axis=0)
    half = lax.broadcasted_iota(jnp.int32, (BAND_ROWS, 128), 1) < WINDOW
    band = jnp.concatenate([jnp.where(half, band, 0.0), jnp.where(half, 0.0, band)], axis=0)
    slot = (lax.broadcasted_iota(jnp.int32, (128, 256), 0) % WINDOW - 16).astype(jnp.float32)
    pick_key = (slot == key_tok).astype(jnp.bfloat16)
    spread = dot(band.astype(jnp.bfloat16), pick_key).astype(jnp.bfloat16)

    row_head = lax.broadcasted_iota(jnp.int32, (128, 128), 0) // QB
    lane_head = lax.broadcasted_iota(jnp.int32, (128, 128), 1) // 32
    own_head = row_head == lane_head
    entry = lax.broadcasted_iota(jnp.int32, (128, WINDOW), 1)
    entry_tok = (2 * ((entry % 32) // 4) + entry // 32).astype(jnp.float32)
    entry_head = entry % 4 == lax.broadcasted_iota(jnp.int32, (128, WINDOW), 0) // QB
    key_lane = lax.broadcasted_iota(jnp.int32, (128, KW), 1)
    for b in range(n_query // QB):
        at = b * QB
        queries = q_scr[at : at + QB, :]
        stacked = jnp.where(own_head, jnp.concatenate([queries] * heads, axis=0), 0)
        keys = k_scr[at : at + KW, :]
        tok_col = col_own[at : at + QB, 0:WINDOW] if at < atoms else col_above[0:QB, 0:WINDOW]
        pick = (jnp.concatenate([tok_col] * heads, axis=0) == entry_tok) & entry_head
        bias = dot(pick.astype(jnp.bfloat16), spread[:, at : at + KW])
        scores = dot_nt(stacked, keys) * (1.0 / math.sqrt(32)) + bias
        key_index = flat * atoms - BELOW + at + key_lane
        scores = jnp.where((key_index >= 0) & (key_index < total), scores, -jnp.inf)
        exponent = jnp.exp(scores - jnp.max(scores, axis=-1, keepdims=True))
        weights = (exponent / jnp.sum(exponent, axis=-1, keepdims=True)).astype(jnp.bfloat16)
        mixed = jnp.where(own_head, dot(weights, v_scr[at : at + KW, :]), 0.0)
        mixed = (mixed[0:32] + mixed[32:64]) + (mixed[64:96] + mixed[96:128])
        gate_scr[at : at + QB, :] = gate_scr[at : at + QB, :] * mixed
    attended = gate_scr[...].astype(jnp.bfloat16)
    atom_out = (wide[BELOW : BELOW + n_query, :] + dot(attended, wout_ref[...])).astype(
        jnp.bfloat16
    )
    atom_out_ref[...] = atom_out[0:atoms]
    next_out_ref[0:16, :] = atom_out[atoms : atoms + 16]
    next_out_ref[16:, :] = jnp.zeros((atoms - 16, 128), jnp.bfloat16)
    shared_ref[...] = col_own.astype(jnp.bfloat16)
    features = jnp.maximum(dot(atom_out, wagg_ref[...]), 0.0)
    tokens = lax.broadcasted_iota(jnp.int32, (TOK_DEV, 128), 0).astype(jnp.float32)
    member = (tok_own == tokens).astype(jnp.float32)
    member_next = ((tok_above == tokens) & (key_lane[0:TOK_DEV] < QB)).astype(jnp.float32)[:, 0:QB]
    counts = jnp.sum(member, axis=1, keepdims=True) + jnp.sum(member_next, axis=1, keepdims=True)
    totals = dot(member, features[0:atoms], precision=lax.Precision.HIGHEST) + dot(
        member_next, features[atoms:], precision=lax.Precision.HIGHEST
    )
    token_single = (totals / counts).astype(jnp.bfloat16)
    token_ref[...] = token_single
    singles = dot(token_single, wsingle_ref[...]).astype(jnp.bfloat16)
    singles_ref[...] = singles


def atom_part(cross, own, tok_rows, near, atom_gain, w_attn, w_out, w_agg, w_single):
    atoms = own.shape[0]
    vmem = pl.BlockSpec(memory_space=pltpu.VMEM)
    return pl.pallas_call(
        atom_kernel,
        in_specs=[vmem] * 9,
        out_specs=[vmem] * 5,
        out_shape=[
            jax.ShapeDtypeStruct((atoms, 128), jnp.bfloat16),
            jax.ShapeDtypeStruct((atoms, 128), jnp.bfloat16),
            jax.ShapeDtypeStruct((atoms, 128), jnp.bfloat16),
            jax.ShapeDtypeStruct((TOK_DEV, 384), jnp.bfloat16),
            jax.ShapeDtypeStruct((TOK_DEV, 256), jnp.bfloat16),
        ],
        scratch_shapes=[
            pltpu.VMEM((atoms + KW, 128), jnp.float32),
            pltpu.VMEM((atoms + QB, 128), jnp.bfloat16),
            pltpu.VMEM((atoms + KW, 128), jnp.bfloat16),
            pltpu.VMEM((atoms + KW, 128), jnp.bfloat16),
            pltpu.VMEM((atoms + QB, 128), jnp.float32),
        ],
        cost_estimate=pl.CostEstimate(flops=10**9, bytes_accessed=10**6, transcendentals=10**5),
        compiler_params=pltpu.CompilerParams(vmem_limit_bytes=16 * MIB),
        name="atoms",
    )(cross, own, tok_rows, near, atom_gain, w_attn, w_out, w_agg, w_single)


def whole(array):
    return pl.BlockSpec(array.shape, lambda i: (0,) * array.ndim)


def halved_gate(w_in_ref, w_in_scr):
    width = w_in_ref.shape[1] // 2
    w_in_scr[:, :width] = w_in_ref[:, :width] * 0.5
    w_in_scr[:, width:] = w_in_ref[:, width:]


def transition(cells, w_in_scr, w_out_ref):
    width = w_out_ref.shape[0]
    wide = cells.reshape(-1, 128).astype(jnp.float32)
    hidden = dot(normalize(wide).astype(jnp.bfloat16), w_in_scr[...])
    gate = hidden[:, :width].astype(jnp.bfloat16)
    up = hidden[:, width:].astype(jnp.bfloat16)
    return wide + dot((gate + gate * jnp.tanh(gate)) * up, w_out_ref[...])


def early_kernel(pair_ref, w_in_ref, w_out_ref, band_ref, out_ref, w_in_scr):
    rows, cols, _ = pair_ref.shape

    @pl.when(pl.program_id(0) == 0)
    def _():
        halved_gate(w_in_ref, w_in_scr)

    step = SUB // cols
    for k in range(0, rows, step):
        moved = transition(pair_ref[k : k + step], w_in_scr, w_out_ref)
        out_ref[k : k + step] = moved.astype(jnp.bfloat16).reshape(step, cols, 128)


def early_part(pair_act, w_in, w_out, band):
    rows, cols, width = pair_act.shape
    block = pl.BlockSpec((EARLY, cols, width), lambda i: (ROWS // EARLY * i, 0, 0))
    cells = rows // ROWS * EARLY * cols
    return pl.pallas_call(
        early_kernel,
        grid=(rows // ROWS,),
        in_specs=[block, whole(w_in), whole(w_out), pl.BlockSpec(memory_space=pl.ANY)],
        out_specs=block,
        out_shape=jax.ShapeDtypeStruct(pair_act.shape, jnp.bfloat16),
        scratch_shapes=[pltpu.VMEM(w_in.shape, jnp.bfloat16)],
        cost_estimate=pl.CostEstimate(
            flops=cells * 196608 * 2, bytes_accessed=cells * 512, transcendentals=0
        ),
        compiler_params=pltpu.CompilerParams(vmem_limit_bytes=WIDE * MIB),
        name="pair_early",
    )(pair_act, w_in, w_out, band)


def last_kernel(
    sender_ref, pair_ref, done_ref, w_in_ref, w_out_ref, own_ref, other_ref, col_ref,
    out_ref, w_in_scr, row_scr, col_scr,
):
    i = pl.program_id(0)
    rows, cols, _ = pair_ref.shape

    @pl.when(i == 0)
    def _():
        halved_gate(w_in_ref, w_in_scr)
        col = lax.axis_index("col")
        sender = sender_ref[lax.axis_index("row") * lax.axis_size("col") + col]
        half = col // 8
        for block in range(8):
            at = slice(block * TOK_DEV, (block + 1) * TOK_DEV)
            row_at = pl.ds(pl.multiple_of((block ^ (col % 8)) * 16, 16), 16)
            col_at = pl.ds(pl.multiple_of((block ^ sender) * 16, 16), 16)
            own_to = pl.ds(pl.multiple_of(half * 128 + block * 16, 16), 16)
            other_to = pl.ds(pl.multiple_of((1 - half) * 128 + block * 16, 16), 16)
            row_scr[own_to, :] = own_ref[row_at, 0:128].astype(jnp.float32)
            row_scr[other_to, :] = other_ref[row_at, 0:128].astype(jnp.float32)
            col_scr[at, :] = col_ref[col_at, 128:256].astype(jnp.float32)

    base = pl.multiple_of(i * rows, rows)
    col_add = col_scr[...]
    step = SUB // cols
    for k in range(EARLY, rows, step):
        moved = transition(pair_ref[k : k + step], w_in_scr, w_out_ref)
        for s in range(step):
            extra = row_scr[pl.ds(base + k + s, 1), :] + col_add
            out_ref[k + s] = (moved[s * cols : (s + 1) * cols] + extra).astype(jnp.bfloat16)
    for r in range(EARLY):
        extra = row_scr[pl.ds(base + r, 1), :] + col_add
        out_ref[r] = (done_ref[r].astype(jnp.float32) + extra).astype(jnp.bfloat16)


def last_part(senders, pair_act, done, w_in, w_out, own, other, col):
    rows, cols, width = pair_act.shape
    block = pl.BlockSpec((ROWS, cols, width), lambda i: (i, 0, 0))
    done_block = pl.BlockSpec((EARLY, cols, width), lambda i: (ROWS // EARLY * i, 0, 0))
    return pl.pallas_call(
        last_kernel,
        grid=(rows // ROWS,),
        in_specs=[pl.BlockSpec(memory_space=pltpu.SMEM), block, done_block]
        + [whole(x) for x in (w_in, w_out, own, other, col)],
        out_specs=block,
        out_shape=jax.ShapeDtypeStruct(pair_act.shape, jnp.bfloat16),
        scratch_shapes=[
            pltpu.VMEM(w_in.shape, jnp.bfloat16),
            pltpu.VMEM((rows, width), jnp.float32),
            pltpu.VMEM((cols, width), jnp.float32),
        ],
        cost_estimate=pl.CostEstimate(
            flops=rows * cols * 196608 * 2, bytes_accessed=rows * cols * 512, transcendentals=0
        ),
        compiler_params=pltpu.CompilerParams(vmem_limit_bytes=WIDE * MIB),
        name="pair_last",
    )(senders, pair_act, done, w_in, w_out, own, other, col)


def chip_of(row, col):
    x_lo, z = divmod(row, 4)
    y, rest = divmod(col, 4)
    return (2 * (rest // 2) + x_lo, y, z)


def hops(one, other):
    return sum(min((a - b) % 4, (b - a) % 4) for a, b in zip(one, other))


def assigned(costs, most):
    owner = {}

    def place(source, seen):
        for target in sorted(range(len(costs)), key=lambda t: costs[source][t]):
            if costs[source][target] <= most and target not in seen:
                seen.add(target)
                if target not in owner or place(owner[target], seen):
                    owner[target] = source
                    return True
        return False

    for source in range(len(costs)):
        if not place(source, set()):
            return None
    return {source: target for target, source in owner.items()}


def column_turn():
    pairs = []
    for row in range(8):
        for half in range(2):
            column = 2 * row + half
            costs = [
                [hops(chip_of(row, 8 * half + k), chip_of(target, column)) for target in range(8)]
                for k in range(8)
            ]
            most = 0
            while assigned(costs, most) is None:
                most += 1
            found = assigned(costs, most)
            pairs += [(16 * row + 8 * half + k, 16 * found[k] + column) for k in range(8)]
    return pairs


def on_device(
    pair_act, atom_act, atom_token, atom_gain, w_attn, w_out, w_bias, w_trans_in, w_trans_out,
    w_agg, w_single,
):
    atom_n = atom_act.shape[0]
    n_row, n_col = lax.axis_size("row"), lax.axis_size("col")
    devices = n_row * n_col
    both = ("row", "col")
    up = [(i, i + 1) for i in range(devices - 1)]
    firsts = [n_col * i for i in range(1, n_row)]
    ends = [(i - 1, i) for i in firsts] + [(i, i - 1) for i in firsts]
    turn = column_turn()
    senders = np.zeros(devices, np.int32)
    for source, target in turn:
        senders[target] = source % 8

    band, cross, tok_rows = band_biases(pair_act, w_bias, atom_act, atom_token)
    cross = lax.ppermute(cross, both, ends)
    near = lax.all_to_all(band, "col", 0, 0, tiled=True)
    done = early_part(pair_act, w_trans_in, w_trans_out, band)
    near, cross = lax.optimization_barrier((near, cross, done))[:2]
    atom_main, next_out, shared, token_single, singles = atom_part(
        cross, atom_act, tok_rows, near, atom_gain[None, :], w_attn, w_out, w_agg, w_single
    )
    def swapped(value, bits):
        return lax.ppermute(value, "col", [(i, i ^ bits) for i in range(n_col)])

    held = jnp.concatenate([singles, swapped(singles, 1)])
    held = jnp.concatenate([held] + [swapped(held, bits) for bits in (2, 4, 6)])
    col_all = lax.ppermute(held, both, turn)
    other = lax.ppermute(held, "col", [(i, i ^ 8) for i in range(n_col)])
    from_below = lax.ppermute(next_out, both, up)
    pair_out = last_part(
        jnp.asarray(senders), pair_act, done, w_trans_in, w_trans_out, held, other, col_all
    )
    from_below = lax.optimization_barrier((from_below, pair_out))[0]
    atom_out = jnp.where(shared < 0, from_below, atom_main)
    return (atom_out, token_single, pair_out)


def solution(mesh):
    both = P(("row", "col"), None)
    return jax.shard_map(
        on_device,
        mesh=mesh,
        in_specs=(P("row", "col", None), both, P(("row", "col"))) + (P(),) * 8,
        out_specs=(both, both, P("row", "col", None)),
        check_vma=False,
    )
```

```python
import functools
import math

import jax
import jax.numpy as jnp
import numpy as np
from jax import lax
from jax.experimental import pallas as pl
from jax.experimental.pallas import tpu as pltpu
from jax.sharding import PartitionSpec as P

SPAN = 10
QB = 32
KW = 128
TOK_DEV = 16
BELOW = (KW - QB) // 2
ABOVE = KW - BELOW
WINDOW = 64
GROUPS = 9
BAND_ROWS = 32
EDGE = 48
BLOCK_ROWS = BAND_ROWS + 16 + ABOVE
BATCH = 3
MIB = 1024 * 1024
WIDE = 50
ROWS = 64
EARLY = 32
SUB = 512


def normalize(values):
    centre = values - jnp.mean(values, axis=-1, keepdims=True)
    spread = jnp.mean(centre * centre, axis=-1, keepdims=True)
    return centre * lax.rsqrt(spread + 1e-05)


def dot(a, b, **kw):
    return jnp.dot(a, b, preferred_element_type=jnp.float32, **kw)


def dot_nt(a, b):
    return lax.dot_general(a, b, (((1,), (1,)), ((), ())), preferred_element_type=jnp.float32)


def band_kernel(
    pair_ref, weight_hbm, atom_hbm, token_hbm, out_ref, cross_ref, tok_ref, cells, weight_ref,
    atom_ref, token_ref, sems, small_sems,
):
    row, col = lax.axis_index("row"), lax.axis_index("col")
    flat_index = row * lax.axis_size("col") + col
    shift = col - 2 * row
    first = jnp.clip(8 * shift - 1, 0, 7)
    small = [
        pltpu.make_async_copy(source, target, small_sems.at[i])
        for i, (source, target) in enumerate(
            [(atom_hbm, atom_ref), (token_hbm, token_ref), (weight_hbm, weight_ref)]
        )
    ]
    for copy in small:
        copy.start()
    copies = []
    for j in range(GROUPS):
        group = first + j
        start = group - 8 * shift - 1
        begin = jnp.clip(start, 0, 4)
        at = jnp.clip(EDGE // 16 + begin - start, 0, 2 * EDGE // 16)
        copy = pltpu.make_async_copy(
            pair_ref.at[
                pl.ds(pl.multiple_of(group * 16, 16), 16),
                pl.ds(pl.multiple_of(begin * 16, 16), WINDOW),
                :,
            ],
            cells.at[j, :, pl.ds(pl.multiple_of(at * 16, 16), WINDOW), :],
            sems.at[j],
        )
        copy.start()
        copies.append(copy)
    out_ref[:, 0:BAND_ROWS, :] = jnp.zeros((out_ref.shape[0], BAND_ROWS, 128), jnp.bfloat16)
    for copy in small:
        copy.wait()
    atoms = atom_ref.shape[0]
    token_rel = (token_ref[...] - flat_index * TOK_DEV).astype(jnp.float32)
    tok_rows = jnp.broadcast_to(token_rel, (16, 128)).astype(jnp.bfloat16)
    tok_ref[...] = tok_rows
    low = BAND_ROWS
    last = out_ref.shape[0] - 1

    def to_above(ref, at):
        ref[at : at + 16, :] = tok_rows
        ref[at + 16 : at + 16 + BELOW, :] = atom_ref[atoms - BELOW :, :]

    def to_below(ref, at):
        ref[at : at + 16, :] = tok_rows
        ref[at + 16 : at + 16 + ABOVE, :] = atom_ref[0:ABOVE, :]

    to_above(out_ref.at[jnp.minimum(col + 1, last)], low)
    to_below(out_ref.at[jnp.maximum(col - 1, 0)], low)

    @pl.when(col == last)
    def _():
        to_above(cross_ref, 0)
        to_below(out_ref.at[last - 1], low)

    @pl.when(col == 0)
    def _():
        to_below(cross_ref, 0)
        to_above(out_ref.at[1], low)

    weight = jnp.concatenate(
        [weight_ref[...].astype(jnp.float32), jnp.zeros((12, 128), jnp.float32)], axis=0
    ).astype(jnp.bfloat16)
    lane_piece = (lax.broadcasted_iota(jnp.int32, (BAND_ROWS, 128), 1) % WINDOW) // 16
    for j0 in range(0, GROUPS, BATCH):
        for j in range(j0, j0 + BATCH):
            copies[j].wait()
        flat = cells[j0 : j0 + BATCH, :, EDGE : EDGE + WINDOW, :].reshape(-1, 128)
        normed = normalize(flat.astype(jnp.float32)).astype(jnp.bfloat16)
        biases = dot_nt(weight, normed)
        for j in range(j0, j0 + BATCH):
            off = (j - j0) * 8
            rows = jnp.concatenate(
                [biases[0:4, 128 * (off + i) : 128 * (off + i + 1)] for i in range(8)], axis=0
            )
            at = first + j - 8 * shift - 1 + lane_piece
            kept = jnp.where((at >= 0) & (at <= 7), rows, 0.0)
            out_ref[pl.ds(first + j, 1), 0:BAND_ROWS, :] = kept.astype(jnp.bfloat16)[None]


def band_biases(pair_act, w_bias, atom_act, atom_token):
    vmem = pl.BlockSpec(memory_space=pltpu.VMEM)
    return pl.pallas_call(
        band_kernel,
        in_specs=[pl.BlockSpec(memory_space=pltpu.HBM)] * 4,
        out_specs=[vmem] * 3,
        out_shape=[
            jax.ShapeDtypeStruct((16, BLOCK_ROWS, 128), jnp.bfloat16),
            jax.ShapeDtypeStruct((16 + ABOVE, 128), jnp.bfloat16),
            jax.ShapeDtypeStruct((16, 128), jnp.bfloat16),
        ],
        scratch_shapes=[
            pltpu.VMEM((GROUPS, 16, WINDOW + 2 * EDGE, 128), jnp.bfloat16),
            pltpu.VMEM((4, 128), jnp.bfloat16),
            pltpu.VMEM(atom_act.shape, jnp.bfloat16),
            pltpu.VMEM((1, atom_act.shape[0]), jnp.int32),
            pltpu.SemaphoreType.DMA((GROUPS,)),
            pltpu.SemaphoreType.DMA((3,)),
        ],
        cost_estimate=pl.CostEstimate(flops=10**9, bytes_accessed=3 * 10**6, transcendentals=0),
        compiler_params=pltpu.CompilerParams(vmem_limit_bytes=56 * MIB),
        name="band",
    )(pair_act, w_bias.T, atom_act, atom_token[None, :])


def atom_kernel(
    cross_ref, own_ref, tok_ref, near_ref, gain_ref, wattn_ref, wout_ref,
    wagg_ref, wsingle_ref, atom_out_ref, next_out_ref, shared_ref, token_ref, singles_ref,
    wide, q_scr, k_scr, v_scr, gate_scr,
):
    n_col = lax.axis_size("col")
    col = lax.axis_index("col")
    flat = lax.axis_index("row") * n_col + col
    atoms = own_ref.shape[0]
    heads = 4
    n_query = atoms + QB
    total = lax.axis_size("row") * n_col * atoms
    last = near_ref.shape[0] - 1
    low = BAND_ROWS
    from_below = near_ref[jnp.maximum(col - 1, 0), low : low + 16 + BELOW, :].astype(jnp.float32)
    from_above = near_ref[jnp.minimum(col + 1, last), low:, :].astype(jnp.float32)
    cross = cross_ref[...].astype(jnp.float32)
    from_below = jnp.where(col == 0, cross[0 : 16 + BELOW], from_below)
    from_above = jnp.where(col == last, cross, from_above)
    wide[0:BELOW, :] = from_below[16:]
    wide[BELOW : BELOW + atoms, :] = own_ref[...].astype(jnp.float32)
    wide[BELOW + atoms :, :] = from_above[16:]
    normed = (normalize(wide[...]) * gain_ref[...]).astype(jnp.bfloat16)
    projected = dot(normed, wattn_ref[...])
    q_scr[...] = projected[BELOW : BELOW + n_query, 0:128].astype(jnp.bfloat16)
    k_scr[...] = projected[:, 128:256].astype(jnp.bfloat16)
    v_scr[...] = projected[:, 256:384].astype(jnp.bfloat16)
    gate_scr[...] = jax.nn.sigmoid(projected[BELOW : BELOW + n_query, 384:512])

    tok_own = tok_ref[0:1, :].astype(jnp.float32)
    tok_below = from_below[0:1] - TOK_DEV
    tok_above = from_above[0:1] + TOK_DEV
    lane = lax.broadcasted_iota(jnp.int32, (8, 128), 1)
    rolled_own = pltpu.roll(jnp.broadcast_to(tok_own, (8, 128)), BELOW, 1)
    rolled_below = pltpu.roll(jnp.broadcast_to(tok_below, (8, 128)), BELOW, 1)
    rolled_above = pltpu.roll(jnp.broadcast_to(tok_above, (8, 128)), BELOW, 1)
    key_tok = jnp.concatenate(
        [
            jnp.where(lane < BELOW, rolled_below, rolled_own)[0:1],
            jnp.where(lane < BELOW, rolled_own, rolled_above)[0:1],
        ],
        axis=1,
    )
    col_own = jnp.transpose(jnp.broadcast_to(tok_own, (128, 128)))
    col_above = jnp.transpose(jnp.broadcast_to(tok_above, (128, 128)))

    band = jnp.sum(near_ref[:, 0:BAND_ROWS, :].astype(jnp.float32), axis=0)
    half = lax.broadcasted_iota(jnp.int32, (BAND_ROWS, 128), 1) < WINDOW
    band = jnp.concatenate([jnp.where(half, band, 0.0), jnp.where(half, 0.0, band)], axis=0)
    slot = (lax.broadcasted_iota(jnp.int32, (128, 256), 0) % WINDOW - 16).astype(jnp.float32)
    pick_key = (slot == key_tok).astype(jnp.bfloat16)
    spread = dot(band.astype(jnp.bfloat16), pick_key).astype(jnp.bfloat16)

    row_head = lax.broadcasted_iota(jnp.int32, (128, 128), 0) // QB
    lane_head = lax.broadcasted_iota(jnp.int32, (128, 128), 1) // 32
    own_head = row_head == lane_head
    entry = lax.broadcasted_iota(jnp.int32, (128, WINDOW), 1)
    entry_tok = (2 * ((entry % 32) // 4) + entry // 32).astype(jnp.float32)
    entry_head = entry % 4 == lax.broadcasted_iota(jnp.int32, (128, WINDOW), 0) // QB
    key_lane = lax.broadcasted_iota(jnp.int32, (128, KW), 1)
    for b in range(n_query // QB):
        at = b * QB
        queries = q_scr[at : at + QB, :]
        stacked = jnp.where(own_head, jnp.concatenate([queries] * heads, axis=0), 0)
        keys = k_scr[at : at + KW, :]
        tok_col = col_own[at : at + QB, 0:WINDOW] if at < atoms else col_above[0:QB, 0:WINDOW]
        pick = (jnp.concatenate([tok_col] * heads, axis=0) == entry_tok) & entry_head
        bias = dot(pick.astype(jnp.bfloat16), spread[:, at : at + KW])
        scores = dot_nt(stacked, keys) * (1.0 / math.sqrt(32)) + bias
        key_index = flat * atoms - BELOW + at + key_lane
        scores = jnp.where((key_index >= 0) & (key_index < total), scores, -jnp.inf)
        exponent = jnp.exp(scores - jnp.max(scores, axis=-1, keepdims=True))
        weights = (exponent / jnp.sum(exponent, axis=-1, keepdims=True)).astype(jnp.bfloat16)
        mixed = jnp.where(own_head, dot(weights, v_scr[at : at + KW, :]), 0.0)
        mixed = (mixed[0:32] + mixed[32:64]) + (mixed[64:96] + mixed[96:128])
        gate_scr[at : at + QB, :] = gate_scr[at : at + QB, :] * mixed
    attended = gate_scr[...].astype(jnp.bfloat16)
    atom_out = (wide[BELOW : BELOW + n_query, :] + dot(attended, wout_ref[...])).astype(
        jnp.bfloat16
    )
    atom_out_ref[...] = atom_out[0:atoms]
    next_out_ref[0:16, :] = atom_out[atoms : atoms + 16]
    next_out_ref[16:, :] = jnp.zeros((atoms - 16, 128), jnp.bfloat16)
    shared_ref[...] = col_own.astype(jnp.bfloat16)
    features = jnp.maximum(dot(atom_out, wagg_ref[...]), 0.0)
    tokens = lax.broadcasted_iota(jnp.int32, (TOK_DEV, 128), 0).astype(jnp.float32)
    member = (tok_own == tokens).astype(jnp.float32)
    member_next = ((tok_above == tokens) & (key_lane[0:TOK_DEV] < QB)).astype(jnp.float32)[:, 0:QB]
    counts = jnp.sum(member, axis=1, keepdims=True) + jnp.sum(member_next, axis=1, keepdims=True)
    totals = dot(member, features[0:atoms], precision=lax.Precision.HIGHEST) + dot(
        member_next, features[atoms:], precision=lax.Precision.HIGHEST
    )
    token_single = (totals / counts).astype(jnp.bfloat16)
    token_ref[...] = token_single
    singles = dot(token_single, wsingle_ref[...]).astype(jnp.bfloat16)
    singles_ref[...] = singles


def atom_part(cross, own, tok_rows, near, atom_gain, w_attn, w_out, w_agg, w_single):
    atoms = own.shape[0]
    vmem = pl.BlockSpec(memory_space=pltpu.VMEM)
    return pl.pallas_call(
        atom_kernel,
        in_specs=[vmem] * 9,
        out_specs=[vmem] * 5,
        out_shape=[
            jax.ShapeDtypeStruct((atoms, 128), jnp.bfloat16),
            jax.ShapeDtypeStruct((atoms, 128), jnp.bfloat16),
            jax.ShapeDtypeStruct((atoms, 128), jnp.bfloat16),
            jax.ShapeDtypeStruct((TOK_DEV, 384), jnp.bfloat16),
            jax.ShapeDtypeStruct((TOK_DEV, 256), jnp.bfloat16),
        ],
        scratch_shapes=[
            pltpu.VMEM((atoms + KW, 128), jnp.float32),
            pltpu.VMEM((atoms + QB, 128), jnp.bfloat16),
            pltpu.VMEM((atoms + KW, 128), jnp.bfloat16),
            pltpu.VMEM((atoms + KW, 128), jnp.bfloat16),
            pltpu.VMEM((atoms + QB, 128), jnp.float32),
        ],
        cost_estimate=pl.CostEstimate(flops=10**9, bytes_accessed=10**6, transcendentals=10**5),
        compiler_params=pltpu.CompilerParams(vmem_limit_bytes=16 * MIB),
        name="atoms",
    )(cross, own, tok_rows, near, atom_gain, w_attn, w_out, w_agg, w_single)


def whole(array):
    return pl.BlockSpec(array.shape, lambda i: (0,) * array.ndim)


def halved_gate(w_in_ref, w_in_scr):
    width = w_in_ref.shape[1] // 2
    w_in_scr[:, :width] = w_in_ref[:, :width] * 0.5
    w_in_scr[:, width:] = w_in_ref[:, width:]


def transition(cells, w_in_scr, w_out_ref):
    width = w_out_ref.shape[0]
    wide = cells.reshape(-1, 128).astype(jnp.float32)
    hidden = dot(normalize(wide).astype(jnp.bfloat16), w_in_scr[...])
    gate = hidden[:, :width].astype(jnp.bfloat16)
    up = hidden[:, width:].astype(jnp.bfloat16)
    return wide + dot((gate + gate * jnp.tanh(gate)) * up, w_out_ref[...])


def early_kernel(pair_ref, w_in_ref, w_out_ref, band_ref, out_ref, w_in_scr):
    rows, cols, _ = pair_ref.shape

    @pl.when(pl.program_id(0) == 0)
    def _():
        halved_gate(w_in_ref, w_in_scr)

    step = SUB // cols
    for k in range(0, rows, step):
        moved = transition(pair_ref[k : k + step], w_in_scr, w_out_ref)
        out_ref[k : k + step] = moved.astype(jnp.bfloat16).reshape(step, cols, 128)


def early_part(pair_act, w_in, w_out, band):
    rows, cols, width = pair_act.shape
    block = pl.BlockSpec((EARLY, cols, width), lambda i: (i, 0, 0))
    cells = ROWS * cols
    return pl.pallas_call(
        early_kernel,
        grid=(ROWS // EARLY,),
        in_specs=[block, whole(w_in), whole(w_out), pl.BlockSpec(memory_space=pl.ANY)],
        out_specs=block,
        out_shape=jax.ShapeDtypeStruct(pair_act.shape, jnp.bfloat16),
        scratch_shapes=[pltpu.VMEM(w_in.shape, jnp.bfloat16)],
        cost_estimate=pl.CostEstimate(
            flops=cells * 196608 * 2, bytes_accessed=cells * 512, transcendentals=0
        ),
        compiler_params=pltpu.CompilerParams(vmem_limit_bytes=WIDE * MIB),
        name="pair_early",
    )(pair_act, w_in, w_out, band)


def last_kernel(
    sender_ref, pair_ref, done_ref, w_in_ref, w_out_ref, own_ref, other_ref, col_ref,
    out_ref, w_in_scr, row_scr, col_scr,
):
    i = pl.program_id(0)
    rows, cols, _ = pair_ref.shape

    @pl.when(i == 0)
    def _():
        halved_gate(w_in_ref, w_in_scr)
        col = lax.axis_index("col")
        sender = sender_ref[lax.axis_index("row") * lax.axis_size("col") + col]
        half = col // 8
        for block in range(8):
            at = slice(block * TOK_DEV, (block + 1) * TOK_DEV)
            row_at = pl.ds(pl.multiple_of((block ^ (col % 8)) * 16, 16), 16)
            col_at = pl.ds(pl.multiple_of((block ^ sender) * 16, 16), 16)
            own_to = pl.ds(pl.multiple_of(half * 128 + block * 16, 16), 16)
            other_to = pl.ds(pl.multiple_of((1 - half) * 128 + block * 16, 16), 16)
            row_scr[own_to, :] = own_ref[row_at, 0:128].astype(jnp.float32)
            row_scr[other_to, :] = other_ref[row_at, 0:128].astype(jnp.float32)
            col_scr[at, :] = col_ref[col_at, 128:256].astype(jnp.float32)

    base = pl.multiple_of(i * rows, rows)
    col_add = col_scr[...]
    step = SUB // cols

    @pl.when(i == 0)
    def _():
        for r in range(rows):
            extra = row_scr[r : r + 1, :] + col_add
            out_ref[r] = (done_ref[r].astype(jnp.float32) + extra).astype(jnp.bfloat16)

    @pl.when(i > 0)
    def _():
        for k in range(0, rows, step):
            moved = transition(pair_ref[k : k + step], w_in_scr, w_out_ref)
            for s in range(step):
                extra = row_scr[pl.ds(base + k + s, 1), :] + col_add
                out_ref[k + s] = (moved[s * cols : (s + 1) * cols] + extra).astype(jnp.bfloat16)


def last_part(senders, pair_act, done, w_in, w_out, own, other, col):
    rows, cols, width = pair_act.shape
    block = pl.BlockSpec((ROWS, cols, width), lambda i: (i, 0, 0))
    done_block = pl.BlockSpec((ROWS, cols, width), lambda i: (0, 0, 0))
    pair_block = pl.BlockSpec((ROWS, cols, width), lambda i: (jnp.maximum(i, 1), 0, 0))
    return pl.pallas_call(
        last_kernel,
        grid=(rows // ROWS,),
        in_specs=[pl.BlockSpec(memory_space=pltpu.SMEM), pair_block, done_block]
        + [whole(x) for x in (w_in, w_out, own, other, col)],
        out_specs=block,
        out_shape=jax.ShapeDtypeStruct(pair_act.shape, jnp.bfloat16),
        scratch_shapes=[
            pltpu.VMEM(w_in.shape, jnp.bfloat16),
            pltpu.VMEM((rows, width), jnp.float32),
            pltpu.VMEM((cols, width), jnp.float32),
        ],
        cost_estimate=pl.CostEstimate(
            flops=rows * cols * 196608 * 2, bytes_accessed=rows * cols * 512, transcendentals=0
        ),
        compiler_params=pltpu.CompilerParams(vmem_limit_bytes=WIDE * MIB),
        name="pair_last",
    )(senders, pair_act, done, w_in, w_out, own, other, col)


def chip_of(row, col):
    x_lo, z = divmod(row, 4)
    y, rest = divmod(col, 4)
    return (2 * (rest // 2) + x_lo, y, z)


def hops(one, other):
    return sum(min((a - b) % 4, (b - a) % 4) for a, b in zip(one, other))


def assigned(costs, most):
    owner = {}

    def place(source, seen):
        for target in sorted(range(len(costs)), key=lambda t: costs[source][t]):
            if costs[source][target] <= most and target not in seen:
                seen.add(target)
                if target not in owner or place(owner[target], seen):
                    owner[target] = source
                    return True
        return False

    for source in range(len(costs)):
        if not place(source, set()):
            return None
    return {source: target for target, source in owner.items()}


def column_turn():
    pairs = []
    for row in range(8):
        for half in range(2):
            column = 2 * row + half
            costs = [
                [hops(chip_of(row, 8 * half + k), chip_of(target, column)) for target in range(8)]
                for k in range(8)
            ]
            most = 0
            while assigned(costs, most) is None:
                most += 1
            found = assigned(costs, most)
            pairs += [(16 * row + 8 * half + k, 16 * found[k] + column) for k in range(8)]
    return pairs


def on_device(
    pair_act, atom_act, atom_token, atom_gain, w_attn, w_out, w_bias, w_trans_in, w_trans_out,
    w_agg, w_single,
):
    atom_n = atom_act.shape[0]
    n_row, n_col = lax.axis_size("row"), lax.axis_size("col")
    devices = n_row * n_col
    both = ("row", "col")
    up = [(i, i + 1) for i in range(devices - 1)]
    firsts = [n_col * i for i in range(1, n_row)]
    ends = [(i - 1, i) for i in firsts] + [(i, i - 1) for i in firsts]
    turn = column_turn()
    senders = np.zeros(devices, np.int32)
    for source, target in turn:
        senders[target] = source % 8

    band, cross, tok_rows = band_biases(pair_act, w_bias, atom_act, atom_token)
    cross = lax.ppermute(cross, both, ends)
    near = lax.all_to_all(band, "col", 0, 0, tiled=True)
    done = early_part(pair_act, w_trans_in, w_trans_out, band)
    near, cross = lax.optimization_barrier((near, cross, done))[:2]
    atom_main, next_out, shared, token_single, singles = atom_part(
        cross, atom_act, tok_rows, near, atom_gain[None, :], w_attn, w_out, w_agg, w_single
    )
    def swapped(value, bits):
        return lax.ppermute(value, "col", [(i, i ^ bits) for i in range(n_col)])

    held = jnp.concatenate([singles, swapped(singles, 1)])
    held = jnp.concatenate([held] + [swapped(held, bits) for bits in (2, 4, 6)])
    col_all = lax.ppermute(held, both, turn)
    other = lax.ppermute(held, "col", [(i, i ^ 8) for i in range(n_col)])
    from_below = lax.ppermute(next_out, both, up)
    pair_out = last_part(
        jnp.asarray(senders), pair_act, done, w_trans_in, w_trans_out, held, other, col_all
    )
    from_below = lax.optimization_barrier((from_below, pair_out))[0]
    atom_out = jnp.where(shared < 0, from_below, atom_main)
    return (atom_out, token_single, pair_out)


def solution(mesh):
    both = P(("row", "col"), None)
    return jax.shard_map(
        on_device,
        mesh=mesh,
        in_specs=(P("row", "col", None), both, P(("row", "col"))) + (P(),) * 8,
        out_specs=(both, both, P("row", "col", None)),
        check_vma=False,
    )
```

```python
import functools
import math

import jax
import jax.numpy as jnp
import numpy as np
from jax import lax
from jax.experimental import pallas as pl
from jax.experimental.pallas import tpu as pltpu
from jax.sharding import PartitionSpec as P

SPAN = 10
QB = 32
KW = 128
TOK_DEV = 16
BELOW = (KW - QB) // 2
ABOVE = KW - BELOW
WINDOW = 64
GROUPS = 9
BAND_ROWS = 32
EDGE = 48
BLOCK_ROWS = BAND_ROWS + 16 + ABOVE
BATCH = 3
MIB = 1024 * 1024
WIDE = 50
ROWS = 64
EARLY = 32
SUB = 512


def normalize(values):
    centre = values - jnp.mean(values, axis=-1, keepdims=True)
    spread = jnp.mean(centre * centre, axis=-1, keepdims=True)
    return centre * lax.rsqrt(spread + 1e-05)


def dot(a, b, **kw):
    return jnp.dot(a, b, preferred_element_type=jnp.float32, **kw)


def dot_nt(a, b):
    return lax.dot_general(a, b, (((1,), (1,)), ((), ())), preferred_element_type=jnp.float32)


def band_kernel(
    pair_ref, weight_hbm, atom_hbm, token_hbm, out_ref, cross_ref, tok_ref, cells, weight_ref,
    atom_ref, token_ref, sems, small_sems,
):
    row, col = lax.axis_index("row"), lax.axis_index("col")
    flat_index = row * lax.axis_size("col") + col
    shift = col - 2 * row
    first = jnp.clip(8 * shift - 1, 0, 7)
    small = [
        pltpu.make_async_copy(source, target, small_sems.at[i])
        for i, (source, target) in enumerate(
            [(atom_hbm, atom_ref), (token_hbm, token_ref), (weight_hbm, weight_ref)]
        )
    ]
    for copy in small:
        copy.start()
    copies = []
    for j in range(GROUPS):
        group = first + j
        start = group - 8 * shift - 1
        begin = jnp.clip(start, 0, 4)
        at = jnp.clip(EDGE // 16 + begin - start, 0, 2 * EDGE // 16)
        copy = pltpu.make_async_copy(
            pair_ref.at[
                pl.ds(pl.multiple_of(group * 16, 16), 16),
                pl.ds(pl.multiple_of(begin * 16, 16), WINDOW),
                :,
            ],
            cells.at[j, :, pl.ds(pl.multiple_of(at * 16, 16), WINDOW), :],
            sems.at[j],
        )
        copy.start()
        copies.append(copy)
    out_ref[:, 0:BAND_ROWS, :] = jnp.zeros((out_ref.shape[0], BAND_ROWS, 128), jnp.bfloat16)
    for copy in small:
        copy.wait()
    atoms = atom_ref.shape[0]
    token_rel = (token_ref[...] - flat_index * TOK_DEV).astype(jnp.float32)
    tok_rows = jnp.broadcast_to(token_rel, (16, 128)).astype(jnp.bfloat16)
    tok_ref[...] = tok_rows
    low = BAND_ROWS
    last = out_ref.shape[0] - 1

    def to_above(ref, at):
        ref[at : at + 16, :] = tok_rows
        ref[at + 16 : at + 16 + BELOW, :] = atom_ref[atoms - BELOW :, :]

    def to_below(ref, at):
        ref[at : at + 16, :] = tok_rows
        ref[at + 16 : at + 16 + ABOVE, :] = atom_ref[0:ABOVE, :]

    to_above(out_ref.at[jnp.minimum(col + 1, last)], low)
    to_below(out_ref.at[jnp.maximum(col - 1, 0)], low)

    @pl.when(col == last)
    def _():
        to_above(cross_ref, 0)
        to_below(out_ref.at[last - 1], low)

    @pl.when(col == 0)
    def _():
        to_below(cross_ref, 0)
        to_above(out_ref.at[1], low)

    weight = jnp.concatenate(
        [weight_ref[...].astype(jnp.float32), jnp.zeros((12, 128), jnp.float32)], axis=0
    ).astype(jnp.bfloat16)
    lane_piece = (lax.broadcasted_iota(jnp.int32, (BAND_ROWS, 128), 1) % WINDOW) // 16
    for j0 in range(0, GROUPS, BATCH):
        for j in range(j0, j0 + BATCH):
            copies[j].wait()
        flat = cells[j0 : j0 + BATCH, :, EDGE : EDGE + WINDOW, :].reshape(-1, 128)
        normed = normalize(flat.astype(jnp.float32)).astype(jnp.bfloat16)
        biases = dot_nt(weight, normed)
        for j in range(j0, j0 + BATCH):
            off = (j - j0) * 8
            rows = jnp.concatenate(
                [biases[0:4, 128 * (off + i) : 128 * (off + i + 1)] for i in range(8)], axis=0
            )
            at = first + j - 8 * shift - 1 + lane_piece
            kept = jnp.where((at >= 0) & (at <= 7), rows, 0.0)
            out_ref[pl.ds(first + j, 1), 0:BAND_ROWS, :] = kept.astype(jnp.bfloat16)[None]


def band_biases(pair_act, w_bias, atom_act, atom_token):
    vmem = pl.BlockSpec(memory_space=pltpu.VMEM)
    return pl.pallas_call(
        band_kernel,
        in_specs=[pl.BlockSpec(memory_space=pltpu.HBM)] * 4,
        out_specs=[vmem] * 3,
        out_shape=[
            jax.ShapeDtypeStruct((16, BLOCK_ROWS, 128), jnp.bfloat16),
            jax.ShapeDtypeStruct((16 + ABOVE, 128), jnp.bfloat16),
            jax.ShapeDtypeStruct((16, 128), jnp.bfloat16),
        ],
        scratch_shapes=[
            pltpu.VMEM((GROUPS, 16, WINDOW + 2 * EDGE, 128), jnp.bfloat16),
            pltpu.VMEM((4, 128), jnp.bfloat16),
            pltpu.VMEM(atom_act.shape, jnp.bfloat16),
            pltpu.VMEM((1, atom_act.shape[0]), jnp.int32),
            pltpu.SemaphoreType.DMA((GROUPS,)),
            pltpu.SemaphoreType.DMA((3,)),
        ],
        cost_estimate=pl.CostEstimate(flops=10**9, bytes_accessed=3 * 10**6, transcendentals=0),
        compiler_params=pltpu.CompilerParams(vmem_limit_bytes=56 * MIB),
        name="band",
    )(pair_act, w_bias.T, atom_act, atom_token[None, :])


def atom_kernel(
    cross_ref, own_ref, tok_ref, near_ref, gain_ref, wattn_ref, wout_ref,
    wagg_ref, wsingle_ref, atom_out_ref, next_out_ref, shared_ref, token_ref, singles_ref,
    wide, q_scr, k_scr, v_scr, gate_scr,
):
    n_col = lax.axis_size("col")
    col = lax.axis_index("col")
    flat = lax.axis_index("row") * n_col + col
    atoms = own_ref.shape[0]
    heads = 4
    n_query = atoms + QB
    total = lax.axis_size("row") * n_col * atoms
    last = near_ref.shape[0] - 1
    low = BAND_ROWS
    from_below = near_ref[jnp.maximum(col - 1, 0), low : low + 16 + BELOW, :].astype(jnp.float32)
    from_above = near_ref[jnp.minimum(col + 1, last), low:, :].astype(jnp.float32)
    cross = cross_ref[...].astype(jnp.float32)
    from_below = jnp.where(col == 0, cross[0 : 16 + BELOW], from_below)
    from_above = jnp.where(col == last, cross, from_above)
    wide[0:BELOW, :] = from_below[16:]
    wide[BELOW : BELOW + atoms, :] = own_ref[...].astype(jnp.float32)
    wide[BELOW + atoms :, :] = from_above[16:]
    normed = (normalize(wide[...]) * gain_ref[...]).astype(jnp.bfloat16)
    projected = dot(normed, wattn_ref[...])
    q_scr[...] = projected[BELOW : BELOW + n_query, 0:128].astype(jnp.bfloat16)
    k_scr[...] = projected[:, 128:256].astype(jnp.bfloat16)
    v_scr[...] = projected[:, 256:384].astype(jnp.bfloat16)
    gate_scr[...] = jax.nn.sigmoid(projected[BELOW : BELOW + n_query, 384:512])

    tok_own = tok_ref[0:1, :].astype(jnp.float32)
    tok_below = from_below[0:1] - TOK_DEV
    tok_above = from_above[0:1] + TOK_DEV
    lane = lax.broadcasted_iota(jnp.int32, (8, 128), 1)
    rolled_own = pltpu.roll(jnp.broadcast_to(tok_own, (8, 128)), BELOW, 1)
    rolled_below = pltpu.roll(jnp.broadcast_to(tok_below, (8, 128)), BELOW, 1)
    rolled_above = pltpu.roll(jnp.broadcast_to(tok_above, (8, 128)), BELOW, 1)
    key_tok = jnp.concatenate(
        [
            jnp.where(lane < BELOW, rolled_below, rolled_own)[0:1],
            jnp.where(lane < BELOW, rolled_own, rolled_above)[0:1],
        ],
        axis=1,
    )
    col_own = jnp.transpose(jnp.broadcast_to(tok_own, (128, 128)))
    col_above = jnp.transpose(jnp.broadcast_to(tok_above, (128, 128)))

    band = jnp.sum(near_ref[:, 0:BAND_ROWS, :].astype(jnp.float32), axis=0)
    half = lax.broadcasted_iota(jnp.int32, (BAND_ROWS, 128), 1) < WINDOW
    band = jnp.concatenate([jnp.where(half, band, 0.0), jnp.where(half, 0.0, band)], axis=0)
    slot = (lax.broadcasted_iota(jnp.int32, (128, 256), 0) % WINDOW - 16).astype(jnp.float32)
    pick_key = (slot == key_tok).astype(jnp.bfloat16)
    spread = dot(band.astype(jnp.bfloat16), pick_key).astype(jnp.bfloat16)

    row_head = lax.broadcasted_iota(jnp.int32, (128, 128), 0) // QB
    lane_head = lax.broadcasted_iota(jnp.int32, (128, 128), 1) // 32
    own_head = row_head == lane_head
    entry = lax.broadcasted_iota(jnp.int32, (128, WINDOW), 1)
    entry_tok = (2 * ((entry % 32) // 4) + entry // 32).astype(jnp.float32)
    entry_head = entry % 4 == lax.broadcasted_iota(jnp.int32, (128, WINDOW), 0) // QB
    key_lane = lax.broadcasted_iota(jnp.int32, (128, KW), 1)
    for b in range(n_query // QB):
        at = b * QB
        queries = q_scr[at : at + QB, :]
        stacked = jnp.where(own_head, jnp.concatenate([queries] * heads, axis=0), 0)
        keys = k_scr[at : at + KW, :]
        tok_col = col_own[at : at + QB, 0:WINDOW] if at < atoms else col_above[0:QB, 0:WINDOW]
        pick = (jnp.concatenate([tok_col] * heads, axis=0) == entry_tok) & entry_head
        bias = dot(pick.astype(jnp.bfloat16), spread[:, at : at + KW])
        scores = dot_nt(stacked, keys) * (1.0 / math.sqrt(32)) + bias
        key_index = flat * atoms - BELOW + at + key_lane
        scores = jnp.where((key_index >= 0) & (key_index < total), scores, -jnp.inf)
        exponent = jnp.exp(scores - jnp.max(scores, axis=-1, keepdims=True))
        weights = (exponent / jnp.sum(exponent, axis=-1, keepdims=True)).astype(jnp.bfloat16)
        mixed = jnp.where(own_head, dot(weights, v_scr[at : at + KW, :]), 0.0)
        mixed = (mixed[0:32] + mixed[32:64]) + (mixed[64:96] + mixed[96:128])
        gate_scr[at : at + QB, :] = gate_scr[at : at + QB, :] * mixed
    attended = gate_scr[...].astype(jnp.bfloat16)
    atom_out = (wide[BELOW : BELOW + n_query, :] + dot(attended, wout_ref[...])).astype(
        jnp.bfloat16
    )
    atom_out_ref[...] = atom_out[0:atoms]
    next_out_ref[0:16, :] = atom_out[atoms : atoms + 16]
    next_out_ref[16:, :] = jnp.zeros((atoms - 16, 128), jnp.bfloat16)
    shared_ref[...] = col_own.astype(jnp.bfloat16)
    features = jnp.maximum(dot(atom_out, wagg_ref[...]), 0.0)
    tokens = lax.broadcasted_iota(jnp.int32, (TOK_DEV, 128), 0).astype(jnp.float32)
    member = (tok_own == tokens).astype(jnp.float32)
    member_next = ((tok_above == tokens) & (key_lane[0:TOK_DEV] < QB)).astype(jnp.float32)[:, 0:QB]
    counts = jnp.sum(member, axis=1, keepdims=True) + jnp.sum(member_next, axis=1, keepdims=True)
    totals = dot(member, features[0:atoms], precision=lax.Precision.HIGHEST) + dot(
        member_next, features[atoms:], precision=lax.Precision.HIGHEST
    )
    token_single = (totals / counts).astype(jnp.bfloat16)
    token_ref[...] = token_single
    singles = dot(token_single, wsingle_ref[...]).astype(jnp.bfloat16)
    singles_ref[...] = singles


def atom_part(cross, own, tok_rows, near, atom_gain, w_attn, w_out, w_agg, w_single):
    atoms = own.shape[0]
    vmem = pl.BlockSpec(memory_space=pltpu.VMEM)
    return pl.pallas_call(
        atom_kernel,
        in_specs=[vmem] * 9,
        out_specs=[vmem] * 5,
        out_shape=[
            jax.ShapeDtypeStruct((atoms, 128), jnp.bfloat16),
            jax.ShapeDtypeStruct((atoms, 128), jnp.bfloat16),
            jax.ShapeDtypeStruct((atoms, 128), jnp.bfloat16),
            jax.ShapeDtypeStruct((TOK_DEV, 384), jnp.bfloat16),
            jax.ShapeDtypeStruct((TOK_DEV, 256), jnp.bfloat16),
        ],
        scratch_shapes=[
            pltpu.VMEM((atoms + KW, 128), jnp.float32),
            pltpu.VMEM((atoms + QB, 128), jnp.bfloat16),
            pltpu.VMEM((atoms + KW, 128), jnp.bfloat16),
            pltpu.VMEM((atoms + KW, 128), jnp.bfloat16),
            pltpu.VMEM((atoms + QB, 128), jnp.float32),
        ],
        cost_estimate=pl.CostEstimate(flops=10**9, bytes_accessed=10**6, transcendentals=10**5),
        compiler_params=pltpu.CompilerParams(vmem_limit_bytes=16 * MIB),
        name="atoms",
    )(cross, own, tok_rows, near, atom_gain, w_attn, w_out, w_agg, w_single)


def whole(array):
    return pl.BlockSpec(array.shape, lambda i: (0,) * array.ndim)


def halved_gate(w_in_ref, w_in_scr):
    width = w_in_ref.shape[1] // 2
    w_in_scr[:, :width] = w_in_ref[:, :width] * 0.5
    w_in_scr[:, width:] = w_in_ref[:, width:]


def transition(cells, w_in_scr, w_out_ref):
    width = w_out_ref.shape[0]
    wide = cells.reshape(-1, 128).astype(jnp.float32)
    hidden = dot(normalize(wide).astype(jnp.bfloat16), w_in_scr[...])
    gate = hidden[:, :width].astype(jnp.bfloat16)
    up = hidden[:, width:].astype(jnp.bfloat16)
    return wide + dot((gate + gate * jnp.tanh(gate)) * up, w_out_ref[...])


def early_kernel(pair_ref, w_in_ref, w_out_ref, band_ref, out_ref, w_in_scr):
    rows, cols, _ = pair_ref.shape

    @pl.when(pl.program_id(0) == 0)
    def _():
        halved_gate(w_in_ref, w_in_scr)

    step = SUB // cols
    for k in range(0, rows, step):
        moved = transition(pair_ref[k : k + step], w_in_scr, w_out_ref)
        out_ref[k : k + step] = moved.astype(jnp.bfloat16).reshape(step, cols, 128)


def early_part(pair_act, w_in, w_out, band):
    rows, cols, width = pair_act.shape
    block = pl.BlockSpec((EARLY, cols, width), lambda i: (i, 0, 0))
    cells = ROWS * cols
    return pl.pallas_call(
        early_kernel,
        grid=(ROWS // EARLY,),
        in_specs=[block, whole(w_in), whole(w_out), pl.BlockSpec(memory_space=pl.ANY)],
        out_specs=block,
        out_shape=jax.ShapeDtypeStruct(pair_act.shape, jnp.bfloat16),
        scratch_shapes=[pltpu.VMEM(w_in.shape, jnp.bfloat16)],
        cost_estimate=pl.CostEstimate(
            flops=cells * 196608 * 2, bytes_accessed=cells * 512, transcendentals=0
        ),
        compiler_params=pltpu.CompilerParams(vmem_limit_bytes=56 * MIB),
        name="pair_early",
    )(pair_act, w_in, w_out, band)


def last_kernel(
    sender_ref, pair_ref, done_ref, w_in_ref, w_out_ref, own_ref, other_ref, col_ref,
    out_ref, w_in_scr, row_scr, col_scr,
):
    i = pl.program_id(0)
    rows, cols, _ = pair_ref.shape

    @pl.when(i == 0)
    def _():
        halved_gate(w_in_ref, w_in_scr)
        col = lax.axis_index("col")
        sender = sender_ref[lax.axis_index("row") * lax.axis_size("col") + col]
        half = col // 8
        for block in range(8):
            at = slice(block * TOK_DEV, (block + 1) * TOK_DEV)
            row_at = pl.ds(pl.multiple_of((block ^ (col % 8)) * 16, 16), 16)
            col_at = pl.ds(pl.multiple_of((block ^ sender) * 16, 16), 16)
            own_to = pl.ds(pl.multiple_of(half * 128 + block * 16, 16), 16)
            other_to = pl.ds(pl.multiple_of((1 - half) * 128 + block * 16, 16), 16)
            row_scr[own_to, :] = own_ref[row_at, 0:128].astype(jnp.float32)
            row_scr[other_to, :] = other_ref[row_at, 0:128].astype(jnp.float32)
            col_scr[at, :] = col_ref[col_at, 128:256].astype(jnp.float32)

    base = pl.multiple_of(i * rows, rows)
    col_add = col_scr[...]
    step = SUB // cols

    @pl.when(i == 0)
    def _():
        for r in range(rows):
            extra = row_scr[r : r + 1, :] + col_add
            out_ref[r] = (done_ref[r].astype(jnp.float32) + extra).astype(jnp.bfloat16)

    @pl.when(i > 0)
    def _():
        for k in range(0, rows, step):
            moved = transition(pair_ref[k : k + step], w_in_scr, w_out_ref)
            for s in range(step):
                extra = row_scr[pl.ds(base + k + s, 1), :] + col_add
                out_ref[k + s] = (moved[s * cols : (s + 1) * cols] + extra).astype(jnp.bfloat16)


def last_part(senders, pair_act, done, w_in, w_out, own, other, col):
    rows, cols, width = pair_act.shape
    block = pl.BlockSpec((ROWS, cols, width), lambda i: (i, 0, 0))
    done_block = pl.BlockSpec((ROWS, cols, width), lambda i: (0, 0, 0))
    pair_block = pl.BlockSpec((ROWS, cols, width), lambda i: (jnp.maximum(i, 1), 0, 0))
    return pl.pallas_call(
        last_kernel,
        grid=(rows // ROWS,),
        in_specs=[pl.BlockSpec(memory_space=pltpu.SMEM), pair_block, done_block]
        + [whole(x) for x in (w_in, w_out, own, other, col)],
        out_specs=block,
        out_shape=jax.ShapeDtypeStruct(pair_act.shape, jnp.bfloat16),
        scratch_shapes=[
            pltpu.VMEM(w_in.shape, jnp.bfloat16),
            pltpu.VMEM((rows, width), jnp.float32),
            pltpu.VMEM((cols, width), jnp.float32),
        ],
        cost_estimate=pl.CostEstimate(
            flops=rows * cols * 196608 * 2, bytes_accessed=rows * cols * 512, transcendentals=0
        ),
        compiler_params=pltpu.CompilerParams(vmem_limit_bytes=WIDE * MIB),
        name="pair_last",
    )(senders, pair_act, done, w_in, w_out, own, other, col)


def chip_of(row, col):
    x_lo, z = divmod(row, 4)
    y, rest = divmod(col, 4)
    return (2 * (rest // 2) + x_lo, y, z)


def hops(one, other):
    return sum(min((a - b) % 4, (b - a) % 4) for a, b in zip(one, other))


def assigned(costs, most):
    owner = {}

    def place(source, seen):
        for target in sorted(range(len(costs)), key=lambda t: costs[source][t]):
            if costs[source][target] <= most and target not in seen:
                seen.add(target)
                if target not in owner or place(owner[target], seen):
                    owner[target] = source
                    return True
        return False

    for source in range(len(costs)):
        if not place(source, set()):
            return None
    return {source: target for target, source in owner.items()}


def column_turn():
    pairs = []
    for row in range(8):
        for half in range(2):
            column = 2 * row + half
            costs = [
                [hops(chip_of(row, 8 * half + k), chip_of(target, column)) for target in range(8)]
                for k in range(8)
            ]
            most = 0
            while assigned(costs, most) is None:
                most += 1
            found = assigned(costs, most)
            pairs += [(16 * row + 8 * half + k, 16 * found[k] + column) for k in range(8)]
    return pairs


def on_device(
    pair_act, atom_act, atom_token, atom_gain, w_attn, w_out, w_bias, w_trans_in, w_trans_out,
    w_agg, w_single,
):
    atom_n = atom_act.shape[0]
    n_row, n_col = lax.axis_size("row"), lax.axis_size("col")
    devices = n_row * n_col
    both = ("row", "col")
    up = [(i, i + 1) for i in range(devices - 1)]
    firsts = [n_col * i for i in range(1, n_row)]
    ends = [(i - 1, i) for i in firsts] + [(i, i - 1) for i in firsts]
    turn = column_turn()
    senders = np.zeros(devices, np.int32)
    for source, target in turn:
        senders[target] = source % 8

    band, cross, tok_rows = band_biases(pair_act, w_bias, atom_act, atom_token)
    cross = lax.ppermute(cross, both, ends)
    near = lax.all_to_all(band, "col", 0, 0, tiled=True)
    done = early_part(pair_act, w_trans_in, w_trans_out, band)
    near, cross = lax.optimization_barrier((near, cross, done))[:2]
    atom_main, next_out, shared, token_single, singles = atom_part(
        cross, atom_act, tok_rows, near, atom_gain[None, :], w_attn, w_out, w_agg, w_single
    )
    def swapped(value, bits):
        return lax.ppermute(value, "col", [(i, i ^ bits) for i in range(n_col)])

    held = jnp.concatenate([singles, swapped(singles, 1)])
    held = jnp.concatenate([held] + [swapped(held, bits) for bits in (2, 4, 6)])
    col_all = lax.ppermute(held, both, turn)
    other = lax.ppermute(held, "col", [(i, i ^ 8) for i in range(n_col)])
    from_below = lax.ppermute(next_out, both, up)
    pair_out = last_part(
        jnp.asarray(senders), pair_act, done, w_trans_in, w_trans_out, held, other, col_all
    )
    from_below = lax.optimization_barrier((from_below, pair_out))[0]
    atom_out = jnp.where(shared < 0, from_below, atom_main)
    return (atom_out, token_single, pair_out)


def solution(mesh):
    both = P(("row", "col"), None)
    return jax.shard_map(
        on_device,
        mesh=mesh,
        in_specs=(P("row", "col", None), both, P(("row", "col"))) + (P(),) * 8,
        out_specs=(both, both, P("row", "col", None)),
        check_vma=False,
    )
```
